256 devices in a mesh: dp: 4 (over y), expert: 64 (over x, z, core).
Axes of the slice: x: 4, y: 4, z: 8, core: 2. Of those that a mesh axis runs over, the one named last changes fastest.
Arguments:
- tokens: bfloat16 [8192, 2048], P(('dp', 'expert')), may hold values from -6 to 6
- expert_ids: int32 [8192, 8], P(('dp', 'expert')), may hold values from 0 to 63, all different within a row; in each aligned block of 32 rows (0 to 31, 32 to 63, ...) at most 6 rows name the same one
- route_gates: float32 [8192, 8], P(('dp', 'expert')), may hold values from 0.05 to 0.5
- gate_up: bfloat16 [64, 768, 2, 2048], P('expert', 'dp'), may hold values from -0.125 to 0.125
- down_weight: bfloat16 [64, 768, 2048], P('expert', 'dp'), may hold values from -0.21875 to 0.21875
- out_grad: bfloat16 [8192, 2048], P(('dp', 'expert')), may hold values from -6 to 6
Outputs:
- moe_out: bfloat16 [8192, 2048], P(('dp', 'expert'))
- gate_grad: float32 [8192, 8], P(('dp', 'expert'))
- token_grad: bfloat16 [8192, 2048], P(('dp', 'expert'))
- gate_up_grad: float32 [64, 768, 2, 2048], P('expert', 'dp')
- down_grad: float32 [64, 768, 2048], P('expert', 'dp')
The draws below stay inside these ranges and needn't reach their ends.
Inputs may be any that keep to these rules, and one draw needn't show every extreme that they name: `expert_ids`: the rows of one device name no expert more than 6 times; in some device's rows some expert is named exactly 6 times. Each row names 8 different experts.
All inputs are finite; a program needn't handle non-finite values.
Results may differ from the reference program's by a relative error of at most 0.012.
Values may be sent and summed in bfloat16 or wider, within the bound.
No kernel may reach another device: no remote copies, remote signals or barrier semaphores. Data moves between devices by JAX's collectives and lax.ppermute only.
A program may use at most 128 MiB of HBM per device.

```python
import math
import jax
import jax.numpy as jnp
import numpy as np
from jax import lax

D = 2048
FF = 768
TOP = 8
TOK_DEV = 32
EXPERTS = 64
TOKENS = 8192
CAP = 6
N_DP = 4
N_EXPERT = 64


def steps_of(rng, dims, cuts, smallest, top_value):
    def one(position, parts):
        heights = jax.random.uniform(jax.random.fold_in(jax.random.fold_in(rng, 6), position), (parts,), jnp.float32, smallest / len(cuts), top_value / len(cuts))
        return jnp.repeat(jnp.exp(heights), dims[position] // parts).reshape((-1,) + (1,) * (len(dims) - position - 1))

    factor_of = one(*cuts[0])
    for cut in cuts[1:]:
        factor_of = factor_of * one(*cut)
    return factor_of


def assign_block(key, own, number, rows, count, top, most, slope):
    order = jax.random.permutation(key, count)
    packed, usual = shares(count, rows * top, most, slope, True), shares(count, rows * top, most, slope, False)
    places = jnp.arange(count)

    def named(tallies, turn):
        used = int((tallies > 0).sum())
        fixed = max(1, used // 4)
        passed = fixed + (places - fixed + turn * (used - fixed)) % max(1, count - fixed)
        return jnp.zeros((count,), jnp.int32).at[order[jnp.where(places < fixed, places, passed)]].set(jnp.asarray(tallies, jnp.int32))

    tallies = jnp.where(number % 4 == 0, named(packed, number // 4), named(usual, number - number // 4 - 1))
    mixed = jax.random.permutation(jax.random.fold_in(own, 3), count)
    donor, receiver = mixed[0:count // 2 * 2:2], mixed[1:count // 2 * 2:2]
    room = jnp.minimum(tallies[donor] - 1, most - tallies[receiver]) // 2
    room = jnp.where((donor == order[0]) | (receiver == order[0]) | (tallies[receiver] == 0), 0, jnp.maximum(room, 0))
    passed = jax.random.randint(jax.random.fold_in(own, 4), (count // 2,), 0, 1 << 20) % (room + 1)
    tallies = tallies.at[donor].add(-passed).at[receiver].add(passed)
    labels = jnp.searchsorted(jnp.cumsum(tallies), jnp.arange(rows * top), side="right").astype(jnp.int32)
    listing = labels.reshape(top, rows).T
    listing = listing[jax.random.permutation(jax.random.fold_in(own, 1), rows)]
    turn = jax.random.randint(jax.random.fold_in(own, 2), (rows, 1), 0, top)
    return jnp.take_along_axis(listing, (jnp.arange(top)[None, :] + turn) % top, axis=1)


def shares(number_of, total, reach, skew, full):
    weights = [(1 << 20) // math.isqrt(grade ** skew) + 1 for grade in range(1, number_of + 1)]
    largest = reach if full else min(reach, max(-(-total // number_of), total * weights[0] // sum(weights)))
    least = 1 if total - largest >= number_of - 1 else 0
    given, spare = [largest] + [least] * (number_of - 1), total - largest - least * (number_of - 1)
    while spare > 0:
        movable = [i for i in range(1, number_of) if given[i] < largest] or [i for i in range(1, number_of) if given[i] < reach]
        whole, left = sum([weights[i] for i in movable]), spare
        for i in movable:
            extra = min(reach - given[i], max(1, left * weights[i] // whole), spare)
            given[i] = given[i] + extra
            spare = spare - extra
    return np.array(given)


def normal_values(key, dims, width, reach, shards=(), kind=jnp.bfloat16):
    drawn = width * jax.random.normal(key, dims, jnp.float32)
    if shards:
        drawn = drawn * steps_of(key, dims, shards, -0.22, 0.18)
    return jnp.clip(drawn, -reach, reach).astype(kind)


def setup_inputs(seed: int = 0) -> dict:
    key_of = jax.random.split(jax.random.key(seed), 7)
    tokens = normal_values(key_of[0], (TOKENS, D), 1.0, 6.0, ((0, 256),))
    expert_ids_keys = jax.random.split(jax.random.fold_in(key_of[1], 1), TOKENS // TOK_DEV)
    expert_ids_turns = jax.random.permutation(jax.random.fold_in(key_of[1], 3), TOKENS // TOK_DEV)
    expert_ids = jax.vmap(lambda own, number: assign_block(jax.random.fold_in(key_of[1], 2), own, number, TOK_DEV, EXPERTS, TOP, CAP, 2))(expert_ids_keys, expert_ids_turns).reshape((TOKENS, TOP))
    route_gates = jnp.clip(0.05 + 0.45 * jax.random.uniform(key_of[2], (TOKENS, TOP), jnp.float32) ** steps_of(key_of[2], (TOKENS, TOP), ((0, 256),), -0.2, 0.2), 0.05, 0.5)
    gate_up = normal_values(key_of[3], (EXPERTS, FF, 2, D), D ** -0.5, 0.125, ((0, 64), (1, 4)))
    down_weight = normal_values(key_of[4], (EXPERTS, FF, D), FF ** -0.5, 0.21875, ((0, 64), (1, 4)))
    out_grad = normal_values(key_of[5], (TOKENS, D), 1.0, 6.0, ((0, 256),))
    return dict(tokens=tokens, expert_ids=expert_ids, route_gates=route_gates, gate_up=gate_up, down_weight=down_weight, out_grad=out_grad)


def expert_pass(operands):
    rows, cot_rows, row_total, gate_w, up_w, down_w = operands
    slot_count = rows.shape[0]
    model_width = rows.shape[1]
    hidden_size = gate_w.shape[0]
    block_rows = min(128, slot_count)
    block_total = ((row_total + block_rows - 1) // block_rows).astype(jnp.int32)

    def one_block(step_index, loop_state):
        outputs, input_grads, weight_grad = loop_state
        first_row = step_index * block_rows
        rows_blk = lax.dynamic_slice_in_dim(rows, first_row, block_rows, 0)
        cot_blk = lax.dynamic_slice_in_dim(cot_rows, first_row, block_rows, 0)
        gate_pre = jnp.dot(rows_blk, gate_w.T, preferred_element_type=jnp.float32)
        up_pre = jnp.dot(rows_blk, up_w.T, preferred_element_type=jnp.float32)
        sigma = jax.nn.sigmoid(gate_pre)
        silu_val = gate_pre * sigma
        hidden = (silu_val * up_pre).astype(jnp.bfloat16)
        result = jnp.dot(hidden, down_w, preferred_element_type=jnp.float32).astype(jnp.bfloat16)
        hidden_cot = jnp.dot(cot_blk, down_w.T, preferred_element_type=jnp.float32)
        gate_cot = (hidden_cot * up_pre * sigma * (1.0 + gate_pre * (1.0 - sigma))).astype(jnp.bfloat16)
        up_cot = (hidden_cot * silu_val).astype(jnp.bfloat16)
        back_rows = (jnp.dot(gate_cot, gate_w, preferred_element_type=jnp.float32)
                     + jnp.dot(up_cot, up_w, preferred_element_type=jnp.float32)).astype(jnp.bfloat16)
        grad_gate = jnp.dot(gate_cot.T, rows_blk, preferred_element_type=jnp.float32)
        grad_up = jnp.dot(up_cot.T, rows_blk, preferred_element_type=jnp.float32)
        grad_down = jnp.dot(hidden.T, cot_blk, preferred_element_type=jnp.float32)
        weight_grad = weight_grad + jnp.stack([grad_gate, grad_up, grad_down], 1)
        outputs = lax.dynamic_update_slice_in_dim(outputs, result, first_row, 0)
        input_grads = lax.dynamic_update_slice_in_dim(input_grads, back_rows, first_row, 0)
        return outputs, input_grads, weight_grad

    initial = (jnp.zeros((slot_count, model_width), jnp.bfloat16),
               jnp.zeros((slot_count, model_width), jnp.bfloat16),
               jnp.zeros((hidden_size, 3, model_width), jnp.float32))
    return lax.fori_loop(jnp.int32(0), block_total, one_block, initial)


def reference(tokens, expert_ids, route_gates, gate_up, down_weight, out_grad):
    group_size = TOK_DEV * N_EXPERT
    slot_count = N_EXPERT * CAP
    route_count = group_size * TOP
    expert_range = jnp.arange(EXPERTS, dtype=jnp.int32)
    route_token = (jnp.arange(route_count, dtype=jnp.int32) // TOP).astype(jnp.int32)
    gate_part = gate_up[:, :, 0, :]
    up_part = gate_up[:, :, 1, :]
    weight_total = jnp.zeros((EXPERTS, FF, 3, D), jnp.float32)
    moe_parts = []
    gate_parts = []
    token_parts = []
    for group_index in range(N_DP):
        lower = group_index * group_size
        group_tokens = tokens[lower:lower + group_size]
        group_ids = expert_ids[lower:lower + group_size]
        group_gates = route_gates[lower:lower + group_size]
        group_cot = out_grad[lower:lower + group_size]
        flat_ids = group_ids.reshape(-1)
        matches = (flat_ids[:, None] == expert_range[None, :]).astype(jnp.int32)
        earlier = (jnp.cumsum(matches, 0) - matches).astype(jnp.int32)
        route_rank = jnp.sum(earlier * matches, 1).astype(jnp.int32)
        target = (flat_ids * slot_count + route_rank).astype(jnp.int32)
        counts = jnp.sum(matches, 0).astype(jnp.int32)
        rows = jnp.zeros((EXPERTS * slot_count, D), jnp.bfloat16).at[target].set(group_tokens[route_token])
        route_cot = (group_gates.reshape(-1)[:, None] * group_cot[route_token].astype(jnp.float32)).astype(jnp.bfloat16)
        cot_rows = jnp.zeros((EXPERTS * slot_count, D), jnp.bfloat16).at[target].set(route_cot)
        outputs, input_grads, weight_grads = lax.map(
            expert_pass,
            (rows.reshape(EXPERTS, slot_count, D), cot_rows.reshape(EXPERTS, slot_count, D),
             counts, gate_part, up_part, down_weight))
        route_out = outputs.reshape(-1, D)[target].reshape(group_size, TOP, D)
        route_dx = input_grads.reshape(-1, D)[target].reshape(group_size, TOP, D)
        moe_parts.append(jnp.sum(group_gates[:, :, None] * route_out.astype(jnp.float32), 1).astype(jnp.bfloat16))
        gate_parts.append(jnp.einsum("td,tkd->tk", group_cot.astype(jnp.float32), route_out.astype(jnp.float32)))
        token_parts.append(jnp.sum(route_dx.astype(jnp.float32), 1).astype(jnp.bfloat16))
        rounded = lax.optimization_barrier(weight_grads.astype(jnp.bfloat16))
        weight_total = weight_total + rounded.astype(jnp.float32)
    moe_out = jnp.concatenate(moe_parts, 0)
    gate_grad = jnp.concatenate(gate_parts, 0)
    token_grad = jnp.concatenate(token_parts, 0)
    gate_up_grad = weight_total[:, :, 0:2, :]
    down_grad = weight_total[:, :, 2, :]
    return moe_out, gate_grad, token_grad, gate_up_grad, down_grad
```

```python
import jax
import jax.numpy as jnp
from jax import lax
from jax.sharding import Mesh
from jax.sharding import PartitionSpec as P

F32 = jnp.float32
BF16 = jnp.bfloat16


def shift(value, axis, step):
    size = lax.axis_size(axis)
    return lax.ppermute(value, axis, [(i, (i + step) % size) for i in range(size)])


def swap(value):
    return lax.ppermute(value, "c", [(0, 1), (1, 0)])


def dot(left, right, left_dim, right_dim):
    return lax.dot_general(
        left, right, (((left_dim,), (right_dim,)), ((), ())), preferred_element_type=F32
    )


def split3(value):
    high = lax.reduce_precision(value, 8, 7)
    rest = value - high
    middle = lax.reduce_precision(rest, 8, 7)
    low = rest - middle
    return [high.astype(BF16), middle.astype(BF16), low.astype(BF16)]


def ring_gather(block):
    size = lax.axis_size("z")
    right = [block]
    left = [block]
    for step in range(size // 2):
        right.append(shift(right[-1], "z", 1))
        if step < size - 1 - size // 2:
            left.append(shift(left[-1], "z", -1))
    return right + left[1:]


def ring_reduce(blocks):
    size = lax.axis_size("z")
    far = size // 2
    right = blocks[: far + 1]
    left = [blocks[0]] + blocks[far + 1 :]
    carry_right = right[far]
    for step in range(far - 1, -1, -1):
        carry_right = shift(carry_right, "z", -1)
        if step:
            carry_right = (carry_right.astype(F32) + right[step].astype(F32)).astype(BF16)
    last = len(left) - 1
    carry_left = left[last]
    for step in range(last - 1, -1, -1):
        carry_left = shift(carry_left, "z", 1)
        if step:
            carry_left = (carry_left.astype(F32) + left[step].astype(F32)).astype(BF16)
    return blocks[0].astype(F32) + carry_right.astype(F32) + carry_left.astype(F32)


def gather_plane(block):
    mine = jnp.concatenate(ring_gather(block), 0)
    return jnp.concatenate([mine, swap(mine)], 0)


def reduce_plane(part):
    half = part.shape[0] // 2
    other = swap(part[half:])
    mine = (part[:half].astype(F32) + other.astype(F32)).astype(BF16)
    return ring_reduce(jnp.split(mine, lax.axis_size("z"), 0))


def body(tokens, expert_ids, route_gates, gate_up, down_weight, out_grad):
    tok_count, model_width = tokens.shape
    top_count = expert_ids.shape[1]
    x_size = lax.axis_size("x")
    z_size = lax.axis_size("z")
    capacity = 6 * 2 * z_size
    units = gate_up.shape[1]
    half = units // 2

    w_gate, w_up, w_down = gate_up[0, :, 0, :], gate_up[0, :, 1, :], down_weight[0]
    own = [
        jnp.concatenate([w_gate[s], w_up[s], w_down[s]], 0)
        for s in (slice(0, half), slice(half, units))
    ]
    before_0 = shift(own[0], "dp", 1)
    after_1 = shift(own[1], "dp", -1)
    before_1 = shift(own[1], "dp", 1)
    after_0 = shift(own[0], "dp", -1)
    far_0 = shift(before_0, "dp", 1)
    far_1 = shift(after_1, "dp", -1)
    near_pieces = [own[0], own[1], before_0, before_1, after_0, after_1]
    far_pieces = [far_0, far_1]

    pad = jnp.zeros((tok_count, 128 - 4 * top_count), BF16)
    payload = jnp.concatenate([tokens, expert_ids.astype(BF16)] + split3(route_gates) + [pad], 1)
    all_tokens = gather_plane(payload)
    all_grads = gather_plane(out_grad)
    held = all_tokens.shape[0]
    info = all_tokens[:, model_width:].astype(F32)
    ids = info[:, :top_count].astype(jnp.int32)
    gates = (
        info[:, top_count : 2 * top_count]
        + info[:, 2 * top_count : 3 * top_count]
        + info[:, 3 * top_count : 4 * top_count]
    )
    x_index = lax.axis_index("x")
    column = lax.axis_index("z") * 2 + lax.axis_index("c")
    offsets = jnp.arange(x_size, dtype=jnp.int32)
    target = ((x_index + offsets) % x_size) * (2 * z_size) + column
    chosen = ids[None, :, :] == target[:, None, None]
    chosen_any = jnp.any(chosen, 2)
    gate_of = jnp.sum(jnp.where(chosen, gates[None], 0.0), 2)
    place = jnp.sum(jnp.where(chosen, jnp.arange(top_count, dtype=jnp.int32), 0), 2)
    earlier = (
        jnp.arange(held, dtype=jnp.int32)[:, None] < jnp.arange(held, dtype=jnp.int32)[None, :]
    ).astype(BF16)
    rank = dot(chosen_any.astype(BF16), earlier, 1, 0).astype(jnp.int32)
    rank = jnp.where(chosen_any, rank, -1)
    slots = jnp.arange(capacity, dtype=jnp.int32)
    hit = rank[:, None, :] == slots[None, :, None]
    slot_gate = jnp.sum(jnp.where(hit, gate_of[:, None, :], 0.0), 2).reshape(-1, 1)
    slot_place = jnp.sum(jnp.where(hit, place[:, None, :], 0), 2).reshape(-1, 1)
    pick = hit.astype(BF16).reshape(x_size * capacity, held)

    def exchange(rows, sign):
        blocks = jnp.split(rows, x_size, 0)
        return jnp.concatenate(
            [blocks[0]] + [shift(blocks[k], "x", sign * k) for k in range(1, x_size)], 0
        )

    rows = exchange(dot(pick, all_tokens[:, :model_width], 1, 0).astype(BF16), 1)
    cots = exchange((slot_gate * dot(pick, all_grads, 1, 0)).astype(BF16), 1)

    def kind(pieces, index):
        return jnp.concatenate([p[index * half : (index + 1) * half] for p in pieces], 0)

    groups = []
    for pieces in (near_pieces, far_pieces):
        g_w, u_w, d_w = kind(pieces, 0), kind(pieces, 1), kind(pieces, 2)
        gate_pre = dot(rows, g_w, 1, 1)
        up_pre = dot(rows, u_w, 1, 1)
        sigma = jax.nn.sigmoid(gate_pre)
        silu = gate_pre * sigma
        hidden = (silu * up_pre).astype(BF16)
        out = dot(hidden, d_w, 1, 0)
        hidden_cot = dot(cots, d_w, 1, 1)
        gate_cot = (hidden_cot * up_pre * sigma * (1.0 + gate_pre * (1.0 - sigma))).astype(BF16)
        up_cot = (hidden_cot * silu).astype(BF16)
        score = jnp.sum(hidden.astype(F32) * hidden_cot, 1, keepdims=True)
        dx = dot(gate_cot, g_w, 1, 0) + dot(up_cot, u_w, 1, 0)
        grads = (
            dot(gate_cot, rows, 0, 0).astype(BF16),
            dot(up_cot, rows, 0, 0).astype(BF16),
            dot(hidden, cots, 0, 0).astype(BF16),
        )
        grad_pieces = [
            jnp.concatenate([g[i * half : (i + 1) * half] for g in grads], 0)
            for i in range(len(pieces))
        ]
        groups.append((out, score, dx, grad_pieces))
    (out_n, score_n, dx_n, grads_n), (out_f, score_f, dx_f, grads_f) = groups

    own_0, own_1, before_g0, before_g1, after_g0, after_g1 = grads_n
    far_g0, far_g1 = grads_f
    relay_0 = shift(far_g0, "dp", 1)
    relay_1 = shift(far_g1, "dp", -1)
    got_before_1 = shift(after_g1, "dp", 1)
    got_after_0 = shift(before_g0, "dp", -1)
    got_before_0 = shift((after_g0.astype(F32) + relay_0.astype(F32)).astype(BF16), "dp", 1)
    got_after_1 = shift((before_g1.astype(F32) + relay_1.astype(F32)).astype(BF16), "dp", -1)
    total_0 = own_0.astype(F32) + got_before_0.astype(F32) + got_after_0.astype(F32)
    total_1 = own_1.astype(F32) + got_before_1.astype(F32) + got_after_1.astype(F32)

    def both(index):
        s = slice(index * half, (index + 1) * half)
        return jnp.concatenate([total_0[s], total_1[s]], 0)

    gate_up_grad = jnp.stack([both(0), both(1)], 1)[None]
    down_grad = both(2)[None]

    route_out = exchange((out_n + out_f).astype(BF16), -1)
    weighted = (slot_gate * route_out.astype(F32)).astype(BF16)
    moe_out = reduce_plane(dot(pick, weighted, 0, 0).astype(BF16)).astype(BF16)

    lanes = jnp.arange(128, dtype=jnp.int32)[None, :]
    s_high, s_middle, s_low = split3(score_n + score_f)
    tail = jnp.where(
        lanes == 0, s_high, jnp.where(lanes == 1, s_middle, jnp.where(lanes == 2, s_low, 0))
    )
    dx_rows = jnp.concatenate([(dx_n + dx_f).astype(BF16), tail.astype(BF16)], 1)
    back = exchange(dx_rows, -1)
    tail = back[:, model_width : model_width + 3].astype(F32)
    score = jnp.sum(tail, 1, keepdims=True) / jnp.where(slot_gate > 0, slot_gate, 1.0)
    spread = jnp.zeros((x_size * capacity, 128), BF16)
    for index, part in enumerate(split3(score)):
        spread = jnp.where(lanes == slot_place + index * top_count, part, spread)
    back = jnp.concatenate([back[:, :model_width], spread], 1)
    summed = reduce_plane(dot(pick, back, 0, 0).astype(BF16))
    token_grad = summed[:, :model_width].astype(BF16)
    tail = summed[:, model_width:]
    gate_grad = (
        tail[:, :top_count]
        + tail[:, top_count : 2 * top_count]
        + tail[:, 2 * top_count : 3 * top_count]
    )
    return moe_out, gate_grad, token_grad, gate_up_grad, down_grad


def solution(mesh):
    wide = Mesh(mesh.devices.reshape(4, 4, 8, 2), ("dp", "x", "z", "c"))
    expert = ("x", "z", "c")
    every = ("dp",) + expert
    in_specs = (
        P(every, None),
        P(every, None),
        P(every, None),
        P(expert, "dp", None, None),
        P(expert, "dp", None),
        P(every, None),
    )
    out_specs = (
        P(every, None),
        P(every, None),
        P(every, None),
        P(expert, "dp", None, None),
        P(expert, "dp", None),
    )
    return jax.shard_map(body, mesh=wide, in_specs=in_specs, out_specs=out_specs, check_vma=False)
```

```python
import functools

import jax
import jax.numpy as jnp
from jax import lax
from jax.experimental import pallas as pl
from jax.experimental.pallas import tpu as pltpu
from jax.sharding import Mesh
from jax.sharding import PartitionSpec as P

F32 = jnp.float32
BF16 = jnp.bfloat16
LANES = 128
TILE = 512
LIMIT = 56 * 1024 * 1024
VMEM = pl.BlockSpec(memory_space=pltpu.VMEM)
SMEM = pl.BlockSpec(memory_space=pltpu.SMEM)
ANY = pl.BlockSpec(memory_space=pl.ANY)


def shift(value, axis, step):
    size = lax.axis_size(axis)
    return lax.ppermute(value, axis, [(i, (i + step) % size) for i in range(size)])


def dot(left, right, left_dim, right_dim):
    return lax.dot_general(
        left, right, (((left_dim,), (right_dim,)), ((), ())), preferred_element_type=F32
    )


def call(kernel, outs, in_specs, out_specs, scratch, flops, bytes_accessed, name):
    return pl.pallas_call(
        kernel,
        out_shape=[jax.ShapeDtypeStruct(s, d) for s, d in outs],
        in_specs=in_specs,
        out_specs=out_specs,
        scratch_shapes=scratch,
        compiler_params=pltpu.CompilerParams(vmem_limit_bytes=LIMIT),
        cost_estimate=pl.CostEstimate(
            flops=flops, bytes_accessed=bytes_accessed, transcendentals=0
        ),
        name=name,
    )


def split3(value):
    high = value.astype(BF16)
    rest = value - high.astype(F32)
    middle = rest.astype(BF16)
    low = (rest - middle.astype(F32)).astype(BF16)
    return high, middle, low


def pack_kernel(tokens, ids, gates, grads, packed):
    width = tokens.shape[1]
    top = ids.shape[1]
    row = lax.broadcasted_iota(jnp.int32, (top, LANES), 0)
    lane = lax.broadcasted_iota(jnp.int32, (top, LANES), 1)
    fields = (ids[...].astype(F32).astype(BF16),) + split3(gates[...])
    tail = jnp.zeros((tokens.shape[0], LANES), F32)
    for index, field in enumerate(fields):
        place = (lane == row + index * top).astype(F32).astype(BF16)
        tail = tail + dot(field, place, 1, 0)
    packed[:, :width] = tokens[...]
    packed[:, width : width + LANES] = tail.astype(BF16)
    packed[:, width + LANES :] = grads[...]


def select_kernel(top, dests, cap, z_index, *refs):
    blocks = refs[:8]
    send, pick_out, gate_out, place_out, held = refs[8:]
    rows = blocks[0].shape[0]
    width = send.shape[2]
    count = rows * len(blocks)
    for index, block in enumerate(blocks):
        held[index * rows : (index + 1) * rows, :] = block[...]
    info = held[:, width : width + LANES].astype(F32).T
    ids = info[:top]
    gates = info[top : 2 * top] + info[2 * top : 3 * top] + info[3 * top : 4 * top]
    order = lax.broadcasted_iota(jnp.int32, (top, count), 0).astype(F32)
    base = (z_index[0] * 2).astype(F32)
    marks, gate_rows, place_rows = [], [], []
    for dest in range(dests):
        expert = base + float((dest // 2) * 16 + dest % 2)
        chosen = ids == expert
        marks.append(jnp.sum(jnp.where(chosen, 1.0, 0.0), 0, keepdims=True))
        gate_rows.append(jnp.sum(jnp.where(chosen, gates, 0.0), 0, keepdims=True))
        place_rows.append(jnp.sum(jnp.where(chosen, order, 0.0), 0, keepdims=True))
    mark = jnp.concatenate(marks, 0)
    before = lax.broadcasted_iota(jnp.int32, (count, count), 0) < lax.broadcasted_iota(
        jnp.int32, (count, count), 1
    )
    rank = dot(mark.astype(BF16), before.astype(F32).astype(BF16), 1, 0)
    rank = jnp.where(mark > 0, rank, -1.0)
    slot = lax.broadcasted_iota(jnp.int32, (cap, count), 0).astype(F32)
    slot_gates = []
    for dest in range(dests):
        span = slice(dest * cap, (dest + 1) * cap)
        hit = rank[dest : dest + 1] == slot
        pick_out[span, :] = jnp.where(hit, 1.0, 0.0).astype(BF16)
        slot_gate = jnp.sum(jnp.where(hit, gate_rows[dest], 0.0), 1, keepdims=True)
        slot_place = jnp.sum(jnp.where(hit, place_rows[dest], 0.0), 1, keepdims=True)
        gate_out[span, :] = jnp.broadcast_to(slot_gate, (cap, LANES))
        place_out[span, :] = jnp.broadcast_to(slot_place, (cap, LANES))
        slot_gates.append(slot_gate)
    slot_gate = jnp.concatenate(slot_gates, 0)

    def columns(step, carry):
        first = pl.multiple_of(step * TILE, TILE)
        second = pl.multiple_of(step * TILE + width + LANES, LANES)
        pick = pick_out[...]
        tok = dot(pick, held[:, pl.ds(first, TILE)], 1, 0).astype(BF16)
        cot = (slot_gate * dot(pick, held[:, pl.ds(second, TILE)], 1, 0)).astype(BF16)
        send[:, :cap, pl.ds(first, TILE)] = tok.reshape(dests, cap, TILE)
        send[:, cap:, pl.ds(first, TILE)] = cot.reshape(dests, cap, TILE)
        return carry

    lax.fori_loop(0, width // TILE, columns, 0)


def expert_kernel(pieces_count, arrived, *refs):
    pieces = refs[:pieces_count]
    result = refs[pieces_count]
    grads = refs[pieces_count + 1 : 2 * pieces_count + 1]
    (x, c, w_gate, w_up, w_down, hid, gcot, ucot, hid_t, gcot_t, ucot_t, score, sems) = refs[
        2 * pieces_count + 1 :
    ]
    dests, double, width = arrived.shape
    cap = double // 2
    count = dests * cap
    half = pieces[0].shape[0] // 3
    units = half * pieces_count
    copies = [
        pltpu.make_async_copy(arrived.at[:, pl.ds(0, cap), :], x, sems.at[0]),
        pltpu.make_async_copy(arrived.at[:, pl.ds(cap, cap), :], c, sems.at[1]),
    ]
    for kind, weight in enumerate((w_gate, w_up, w_down)):
        for index, piece in enumerate(pieces):
            copies.append(
                pltpu.make_async_copy(
                    piece.at[pl.ds(kind * half, half), :],
                    weight.at[pl.ds(index * half, half), :],
                    sems.at[2 + kind * pieces_count + index],
                )
            )
    for copy in copies:
        copy.start()
    for copy in copies:
        copy.wait()
    score[...] = jnp.zeros_like(score)

    def unit_tile(step, carry):
        first = pl.multiple_of(step * 256, 256)
        span = pl.ds(first, 256)
        rows = x[...].reshape(count, width)
        gate_pre = dot(rows, w_gate[span, :], 1, 1)
        up_pre = dot(rows, w_up[span, :], 1, 1)
        hidden_cot = dot(c[...].reshape(count, width), w_down[span, :], 1, 1)
        sigma = jax.nn.sigmoid(gate_pre)
        silu = gate_pre * sigma
        hidden = (silu * up_pre).astype(BF16)
        gate_cot = hidden_cot * up_pre * sigma * (1.0 + gate_pre * (1.0 - sigma))
        up_cot = hidden_cot * silu
        hid[:, span] = hidden
        gcot[:, span] = gate_cot.astype(BF16)
        ucot[:, span] = up_cot.astype(BF16)
        hid_t[span, :] = hidden.astype(F32).T.astype(BF16)
        gcot_t[span, :] = gate_cot.T.astype(BF16)
        ucot_t[span, :] = up_cot.T.astype(BF16)
        both = hidden.astype(F32) * hidden_cot
        score[...] += both[:, :LANES] + both[:, LANES:]
        return carry

    lax.fori_loop(0, units // 256, unit_tile, 0)

    def columns(step, carry):
        first = pl.multiple_of(step * TILE, TILE)
        span = pl.ds(first, TILE)
        out = dot(hid[...], w_down[:, span], 1, 0)
        result[:, :cap, span] = out.astype(BF16).reshape(dests, cap, TILE)
        dx = dot(gcot[...], w_gate[:, span], 1, 0) + dot(ucot[...], w_up[:, span], 1, 0)
        result[:, cap:, span] = dx.astype(BF16).reshape(dests, cap, TILE)
        rows = x[:, :, span].reshape(count, TILE)
        cots = c[:, :, span].reshape(count, TILE)
        for kind, (left, right) in enumerate(((gcot_t, rows), (ucot_t, rows), (hid_t, cots))):
            grad = dot(left[...], right, 1, 0).astype(BF16)
            for index in range(pieces_count):
                grads[index][kind * half : (kind + 1) * half, span] = grad[
                    index * half : (index + 1) * half
                ]
        return carry

    lax.fori_loop(0, width // TILE, columns, 0)
    total = jnp.sum(score[...], 1, keepdims=True)
    lane = lax.broadcasted_iota(jnp.int32, (count, LANES), 1)
    high, middle, low = (part.astype(F32) for part in split3(total))
    tail = jnp.where(lane == 0, high, jnp.where(lane == 1, middle, jnp.where(lane == 2, low, 0.0)))
    result[:, cap:, width:] = tail.astype(BF16).reshape(dests, cap, LANES)
    result[:, :cap, width:] = jnp.zeros((dests, cap, LANES), BF16)


def combine_kernel(top, back, pick, slot_gate, slot_place, *blocks):
    dests, double, wide = back.shape
    width = wide - LANES
    cap = double // 2
    count = dests * cap
    rows = blocks[0].shape[0]
    gate = slot_gate[:, :1]

    def columns(step, carry):
        first = pl.multiple_of(step * TILE, TILE)
        second = pl.multiple_of(step * TILE + width + LANES, LANES)
        out = back[:, :cap, pl.ds(first, TILE)].reshape(count, TILE)
        dx = back[:, cap:, pl.ds(first, TILE)].reshape(count, TILE)
        weighted = (gate * out.astype(F32)).astype(BF16)
        moe = dot(pick[...], weighted, 0, 0).astype(BF16)
        grad = dot(pick[...], dx, 0, 0).astype(BF16)
        for index, block in enumerate(blocks):
            span = slice(index * rows, (index + 1) * rows)
            block[:, pl.ds(first, TILE)] = moe[span]
            block[:, pl.ds(second, TILE)] = grad[span]
        return carry

    lax.fori_loop(0, width // TILE, columns, 0)
    tail = back[:, cap:, width:].reshape(count, LANES).astype(F32)
    total = jnp.sum(tail, 1, keepdims=True) / jnp.where(gate > 0, gate, 1.0)
    lane = lax.broadcasted_iota(jnp.int32, (count, LANES), 1).astype(F32)
    spread = jnp.zeros((count, LANES), F32)
    for index, part in enumerate(split3(total)):
        spread = jnp.where(lane == slot_place[...] + float(index * top), part.astype(F32), spread)
    tail = dot(pick[...], spread.astype(BF16), 0, 0).astype(BF16)
    for index, block in enumerate(blocks):
        block[:, width : width + LANES] = tail[index * rows : (index + 1) * rows]


def ring_gather(block):
    size = lax.axis_size("z")
    right = [block]
    left = [block]
    for step in range(size // 2):
        right.append(shift(right[-1], "z", 1))
        if step < size - 1 - size // 2:
            left.append(shift(left[-1], "z", -1))
    return right + left[1:]


def add(left, right):
    return (left.astype(F32) + right.astype(F32)).astype(BF16)


def ring_reduce(blocks):
    far = lax.axis_size("z") // 2
    right = blocks[: far + 1]
    left = [blocks[0]] + blocks[far + 1 :]
    last = len(left) - 1
    carry_right = right[far]
    carry_left = left[last]
    for step in range(far):
        carry_right = shift(carry_right, "z", -1)
        if step < far - 1:
            carry_right = add(carry_right, right[far - 1 - step])
        if step < last:
            carry_left = shift(carry_left, "z", 1)
            if step < last - 1:
                carry_left = add(carry_left, left[last - 1 - step])
    return blocks[0].astype(F32) + carry_right.astype(F32) + carry_left.astype(F32)


def body(tokens, expert_ids, route_gates, gate_up, down_weight, out_grad):
    tok_count, width = tokens.shape
    top = expert_ids.shape[1]
    z_size = lax.axis_size("z")
    dests = lax.axis_size("x") * 2
    cap = 6 * z_size
    count = dests * cap
    held = tok_count * z_size
    units = gate_up.shape[1]
    half = units // 2
    wide = 2 * width + LANES

    w_gate, w_up, w_down = gate_up[0, :, 0, :], gate_up[0, :, 1, :], down_weight[0]
    own = [
        jnp.concatenate([w_gate[s], w_up[s], w_down[s]], 0)
        for s in (slice(0, half), slice(half, units))
    ]
    before_0 = shift(own[0], "dp", 1)
    after_1 = shift(own[1], "dp", -1)
    before_1 = shift(own[1], "dp", 1)
    after_0 = shift(own[0], "dp", -1)
    far_0 = shift(before_0, "dp", 1)
    far_1 = shift(after_1, "dp", -1)
    pieces = [own[0], own[1], before_0, before_1, after_0, after_1, far_0, far_1]

    (packed,) = call(
        pack_kernel, [((tok_count, wide), BF16)], [VMEM] * 4, [VMEM], [], 10**6, 6 * 10**5, "pack"
    )(tokens, expert_ids, route_gates, out_grad)
    blocks = ring_gather(packed)
    z_index = lax.axis_index("z").astype(jnp.int32).reshape(1)
    send, pick, slot_gate, slot_place = call(
        functools.partial(select_kernel, top, dests, cap),
        [
            ((dests, 2 * cap, width), BF16),
            ((count, held), BF16),
            ((count, LANES), F32),
            ((count, LANES), F32),
        ],
        [SMEM] + [VMEM] * len(blocks),
        [VMEM] * 4,
        [pltpu.VMEM((held, wide), BF16)],
        4 * count * held * width,
        6 * 10**6,
        "select",
    )(z_index, *blocks)
    arrived = lax.all_to_all(send, ("x", "c"), 0, 0, tiled=True)

    n = len(pieces)
    full = n * half
    result, *grads = call(
        functools.partial(expert_kernel, n),
        [((dests, 2 * cap, width + LANES), BF16)] + [((3 * half, width), BF16)] * n,
        [ANY] * (1 + n),
        [VMEM] * (1 + n),
        [pltpu.VMEM((dests, cap, width), BF16)] * 2
        + [pltpu.VMEM((full, width), BF16)] * 3
        + [pltpu.VMEM((count, full), BF16)] * 3
        + [pltpu.VMEM((full, count), BF16)] * 3
        + [pltpu.VMEM((count, LANES), F32), pltpu.SemaphoreType.DMA((2 + 3 * n,))],
        18 * count * full * width,
        25 * 10**6,
        "expert",
    )(arrived, *pieces)

    own_0, own_1, before_g0, before_g1, after_g0, after_g1, far_g0, far_g1 = grads
    relay_0 = shift(far_g0, "dp", 1)
    relay_1 = shift(far_g1, "dp", -1)
    got_before_1 = shift(after_g1, "dp", 1)
    got_after_0 = shift(before_g0, "dp", -1)
    got_before_0 = shift(add(after_g0, relay_0), "dp", 1)
    got_after_1 = shift(add(before_g1, relay_1), "dp", -1)
    total_0 = own_0.astype(F32) + got_before_0.astype(F32) + got_after_0.astype(F32)
    total_1 = own_1.astype(F32) + got_before_1.astype(F32) + got_after_1.astype(F32)

    def both(index):
        s = slice(index * half, (index + 1) * half)
        return jnp.concatenate([total_0[s], total_1[s]], 0)

    gate_up_grad = jnp.stack([both(0), both(1)], 1)[None]
    down_grad = both(2)[None]

    back = lax.all_to_all(result, ("x", "c"), 0, 0, tiled=True)
    parts = call(
        functools.partial(combine_kernel, top),
        [((tok_count, wide), BF16)] * z_size,
        [VMEM] * 4,
        [VMEM] * z_size,
        [],
        4 * count * held * width,
        6 * 10**6,
        "combine",
    )(back, pick, slot_gate, slot_place)
    summed = ring_reduce(list(parts))
    moe_out = summed[:, :width].astype(BF16)
    tail = summed[:, width : width + LANES]
    token_grad = summed[:, width + LANES :].astype(BF16)
    gate_grad = tail[:, :top] + tail[:, top : 2 * top] + tail[:, 2 * top : 3 * top]
    return moe_out, gate_grad, token_grad, gate_up_grad, down_grad


def solution(mesh):
    wide = Mesh(mesh.devices.reshape(4, 4, 8, 2), ("dp", "x", "z", "c"))
    expert = ("x", "z", "c")
    every = ("dp",) + expert
    in_specs = (
        P(every, None),
        P(every, None),
        P(every, None),
        P(expert, "dp", None, None),
        P(expert, "dp", None),
        P(every, None),
    )
    out_specs = (
        P(every, None),
        P(every, None),
        P(every, None),
        P(expert, "dp", None, None),
        P(expert, "dp", None),
    )
    return jax.shard_map(body, mesh=wide, in_specs=in_specs, out_specs=out_specs, check_vma=False)
```

```python
import functools

import jax
import jax.numpy as jnp
from jax import lax
from jax.experimental import pallas as pl
from jax.experimental.pallas import tpu as pltpu
from jax.sharding import Mesh
from jax.sharding import PartitionSpec as P

F32 = jnp.float32
BF16 = jnp.bfloat16
LANES = 128
TILE = 512
PIECES = 5
PLACES = ((0, 0), (0, 3), (1, 0), (1, 3), (2, 0), (2, 3), (3, 0), (4, 0))
MIB = 56
COST = {"pack": 0, "touch2": 0, "weights": 10, "select": 0, "merge": 80, "combine": 0, "combine_cot": 0, "forward": 1, "backward": 1, "final": 0, "touch": 10}
VMEM = pl.BlockSpec(memory_space=pltpu.VMEM)
SMEM = pl.BlockSpec(memory_space=pltpu.SMEM)
ANY = pl.BlockSpec(memory_space=pl.ANY)


def shift(value, axis, step):
    size = lax.axis_size(axis)
    return lax.ppermute(value, axis, [(i, (i + step) % size) for i in range(size)])


def dot(left, right, left_dim, right_dim):
    return lax.dot_general(
        left, right, (((left_dim,), (right_dim,)), ((), ())), preferred_element_type=F32
    )


def call(kernel, outs, in_specs, out_specs, scratch, flops, bytes_accessed, mib, name):
    return pl.pallas_call(
        kernel,
        out_shape=[jax.ShapeDtypeStruct(s, d) for s, d in outs],
        in_specs=in_specs,
        out_specs=out_specs,
        scratch_shapes=scratch,
        compiler_params=pltpu.CompilerParams(vmem_limit_bytes=mib * 1024 * 1024),
        cost_estimate=pl.CostEstimate(
            flops=COST[name] * 10**9, bytes_accessed=0, transcendentals=0
        ),
        name=name,
    )


def split3(value):
    high = value.astype(BF16)
    rest = value - high.astype(F32)
    middle = rest.astype(BF16)
    low = (rest - middle.astype(F32)).astype(BF16)
    return high, middle, low


def pack_kernel(tokens, ids, gates, grads, packed):
    width = tokens.shape[1]
    top = ids.shape[0]
    row = lax.broadcasted_iota(jnp.int32, (top, LANES), 0)
    lane = lax.broadcasted_iota(jnp.int32, (top, LANES), 1)
    fields = (ids[...].astype(F32).astype(BF16),) + split3(gates[...])
    tail = jnp.zeros((tokens.shape[0], LANES), F32)
    for index, field in enumerate(fields):
        place = (lane == row + index * top).astype(F32).astype(BF16)
        tail = tail + dot(field, place, 0, 0)
    packed[:, :width] = tokens[...]
    packed[:, width : width + LANES] = tail.astype(BF16)
    packed[:, width + LANES :] = grads[...]


def weights_kernel(gate_up, down, own):
    half = own.shape[0] // 6
    for part in range(2):
        units = slice(part * half, (part + 1) * half)
        first = 3 * part * half
        for kind in range(2):
            rows = slice(first + kind * half, first + (kind + 1) * half)
            own[rows, :] = gate_up[0, units, kind, :]
        own[first + 2 * half : first + 3 * half, :] = down[0, units, :]


def gather_blocks(blocks, held):
    first = 0
    for block in blocks:
        held[first : first + block.shape[0], :] = block[...]
        first += block.shape[0]


def select_kernel(top, dests, cap, z_index, *refs):
    blocks = refs[:5]
    send, pick_out, gate_out, place_out, held = refs[-5:]
    width = send.shape[2]
    count = held.shape[0]
    gather_blocks(blocks, held)
    info = held[:, width : width + LANES].astype(F32).T
    ids = info[:top]
    gates = info[top : 2 * top] + info[2 * top : 3 * top] + info[3 * top : 4 * top]
    order = lax.broadcasted_iota(jnp.int32, (top, count), 0).astype(F32)
    base = (z_index[0] * 2).astype(F32)
    marks, gate_rows, place_rows = [], [], []
    for dest in range(dests):
        expert = base + float((dest // 2) * 16 + dest % 2)
        chosen = ids == expert
        marks.append(jnp.sum(jnp.where(chosen, 1.0, 0.0), 0, keepdims=True))
        gate_rows.append(jnp.sum(jnp.where(chosen, gates, 0.0), 0, keepdims=True))
        place_rows.append(jnp.sum(jnp.where(chosen, order, 0.0), 0, keepdims=True))
    mark = jnp.concatenate(marks, 0)
    before = lax.broadcasted_iota(jnp.int32, (count, count), 0) < lax.broadcasted_iota(
        jnp.int32, (count, count), 1
    )
    rank = dot(mark.astype(BF16), before.astype(F32).astype(BF16), 1, 0)
    rank = jnp.where(mark > 0, rank, -1.0)
    slot = lax.broadcasted_iota(jnp.int32, (cap, count), 0).astype(F32)
    slot_gates = []
    for dest in range(dests):
        span = slice(dest * cap, (dest + 1) * cap)
        hit = rank[dest : dest + 1] == slot
        pick_out[span, :] = jnp.where(hit, 1.0, 0.0).astype(BF16)
        slot_gate = jnp.sum(jnp.where(hit, gate_rows[dest], 0.0), 1, keepdims=True)
        slot_place = jnp.sum(jnp.where(hit, place_rows[dest], 0.0), 1, keepdims=True)
        gate_out[span, :] = jnp.broadcast_to(slot_gate, (cap, LANES))
        place_out[span, :] = jnp.broadcast_to(slot_place, (cap, LANES))
        slot_gates.append(slot_gate)
    slot_gate = jnp.concatenate(slot_gates, 0)

    def columns(step, carry):
        span = pl.ds(pl.multiple_of(step * TILE, TILE), TILE)
        tok = dot(pick_out[...], held[:, span], 1, 0).astype(BF16)
        send[:, :cap, span] = tok.reshape(dests, cap, TILE)
        second = pl.ds(pl.multiple_of(step * TILE + width + LANES, LANES), TILE)
        cot = slot_gate * dot(pick_out[...], held[:, second], 1, 0)
        send[:, cap:, span] = cot.astype(BF16).reshape(dests, cap, TILE)
        return carry

    lax.fori_loop(0, width // TILE, columns, 0)


def load(pieces, places, weights, sems):
    half = pieces[-1].shape[0] // 3
    copies = []
    for index, (number, first) in enumerate(places):
        group = []
        for slot, (kind, weight) in enumerate(weights):
            copy = pltpu.make_async_copy(
                pieces[number].at[pl.ds(first * half + kind * half, half), :],
                weight.at[pl.ds(index * half, half), :],
                sems.at[index * len(weights) + slot],
            )
            copy.start()
            group.append(copy)
        copies.append(group)
    return copies


def wait_all(copies):
    for group in copies:
        for copy in group:
            copy.wait()


def hidden_parts(gate_pre, up_pre, hidden_cot):
    sigma = jax.nn.sigmoid(gate_pre)
    gate_cot = hidden_cot * up_pre * sigma * (1.0 + gate_pre * (1.0 - sigma))
    return gate_cot, hidden_cot * (gate_pre * sigma)


def fold(value):
    wide = jnp.concatenate([value, jnp.zeros((value.shape[0], 64), F32)], 1)
    return wide[:, :LANES] + wide[:, LANES:]


def forward_kernel(arrived, *refs):
    pieces = refs[:PIECES]
    gate_all, up_all, hid, result, gcot, ucot, score, grad_0, grad_1 = refs[PIECES : PIECES + 9]
    hid_far, lefts, w_gate, w_up, w_down, sems = refs[PIECES + 9 :]
    dests, double, width = arrived.shape
    cap = double // 2
    count = dests * cap
    half = grad_0.shape[0] // 3
    copies = load(pieces, PLACES, ((0, w_gate), (1, w_up), (2, w_down)), sems)
    rows = arrived[:, :cap, :].reshape(count, width)
    shards = len(PLACES) // 2
    hidden = []
    for shard in range(shards):
        wait_all(copies[2 * shard : 2 * shard + 2])
        span = slice(2 * shard * half, 2 * (shard + 1) * half)
        gate_pre = dot(rows, w_gate[span, :], 1, 1)
        up_pre = dot(rows, w_up[span, :], 1, 1)
        value = (gate_pre * jax.nn.sigmoid(gate_pre) * up_pre).astype(BF16)
        if shard < shards - 1:
            gate_all[shard], up_all[shard], hid[shard] = gate_pre, up_pre, value
            hidden.append(hid.at[shard])
    hid_far[...] = value
    hidden.append(hid_far)
    hidden_cot = dot(arrived[:, cap:, :].reshape(count, width), w_down[span, :], 1, 1)
    gate_cot, up_cot = hidden_parts(gate_pre, up_pre, hidden_cot)
    gcot[...] = gate_cot.astype(BF16)
    ucot[...] = up_cot.astype(BF16)
    score[...] = fold(value.astype(F32) * hidden_cot)
    lefts[0] = gate_cot.T.astype(BF16)
    lefts[1] = up_cot.T.astype(BF16)
    lefts[2] = value.astype(F32).T.astype(BF16)
    write_grads(arrived, lefts, (grad_0, grad_1))

    def columns(step, carry):
        span = pl.ds(pl.multiple_of(step * TILE, TILE), TILE)
        out = jnp.zeros((count, TILE), F32)
        for shard, value in enumerate(hidden):
            units = slice(2 * shard * half, 2 * (shard + 1) * half)
            out = out + dot(value[...], w_down[units, span], 1, 0)
        result[:, :, span] = out.astype(BF16).reshape(dests, cap, TILE)
        return carry

    lax.fori_loop(0, width // TILE, columns, 0)


def write_grads(arrived, lefts, pieces):
    dests, double, width = arrived.shape
    cap = double // 2
    count = dests * cap
    half = pieces[0].shape[0] // 3

    def columns(step, carry):
        span = pl.ds(pl.multiple_of(step * TILE, TILE), TILE)
        rows = arrived[:, :cap, span].reshape(count, TILE)
        cots = arrived[:, cap:, span].reshape(count, TILE)
        for kind, right in enumerate((rows, rows, cots)):
            grad = dot(lefts[kind], right, 1, 0).astype(BF16)
            for index, piece in enumerate(pieces):
                piece[kind * half : (kind + 1) * half, span] = grad[
                    index * half : (index + 1) * half
                ]
        return carry

    lax.fori_loop(0, width // TILE, columns, 0)


def backward_kernel(arrived, gate_all, up_all, hid, gcot_far, ucot_far, score_far, *refs):
    pieces = refs[:PIECES]
    near = len(PLACES) - 2
    result = refs[PIECES]
    grads = refs[PIECES + 1 : PIECES + 1 + near]
    gcot, ucot, lefts, w_gate, w_up, w_down, sems = refs[PIECES + 1 + near :]
    dests, double, width = arrived.shape
    cap = double // 2
    count = dests * cap
    half = grads[0].shape[0] // 3
    copies = load(pieces, PLACES[:near], ((2, w_down),), sems.at[pl.ds(0, near)])
    others = load(pieces, PLACES, ((0, w_gate), (1, w_up)), sems.at[pl.ds(near, 2 * near + 4)])
    cots = arrived[:, cap:, :].reshape(count, width)
    score = score_far[...]
    for shard in range(near // 2):
        wait_all(copies[2 * shard : 2 * shard + 2])
        span = slice(2 * shard * half, 2 * (shard + 1) * half)
        hidden_cot = dot(cots, w_down[span, :], 1, 1)
        hidden = hid[shard].astype(F32)
        gate_cot, up_cot = hidden_parts(gate_all[shard], up_all[shard], hidden_cot)
        gcot[shard] = gate_cot.astype(BF16)
        ucot[shard] = up_cot.astype(BF16)
        lefts[0, span, :] = gate_cot.T.astype(BF16)
        lefts[1, span, :] = up_cot.T.astype(BF16)
        lefts[2, span, :] = hidden.T.astype(BF16)
        score = score + fold(hidden * hidden_cot)
    total = jnp.sum(score, 1, keepdims=True)
    lane = lax.broadcasted_iota(jnp.int32, (count, LANES), 1)
    high, middle, low = (part.astype(F32) for part in split3(total))
    tail = jnp.where(lane == 0, high, jnp.where(lane == 1, middle, jnp.where(lane == 2, low, 0.0)))
    result[:, :, width:] = tail.astype(BF16).reshape(dests, cap, LANES)
    write_grads(arrived, lefts, grads)
    wait_all(others)

    def columns(step, carry):
        span = pl.ds(pl.multiple_of(step * TILE, TILE), TILE)
        first = half * near
        dx = dot(gcot_far[...], w_gate[first:, span], 1, 0)
        dx = dx + dot(ucot_far[...], w_up[first:, span], 1, 0)
        for shard in range(near // 2):
            units = slice(2 * shard * half, 2 * (shard + 1) * half)
            dx = dx + dot(gcot[shard], w_gate[units, span], 1, 0)
            dx = dx + dot(ucot[shard], w_up[units, span], 1, 0)
        result[:, :, span] = dx.astype(BF16).reshape(dests, cap, TILE)
        return carry

    lax.fori_loop(0, width // TILE, columns, 0)


def spread_blocks(blocks, value, span):
    first = 0
    for block in blocks:
        block[:, span] = value[first : first + block.shape[0]]
        first += block.shape[0]


def combine_kernel(back, pick, slot_gate, joined, *blocks):
    del joined
    dests, cap, width = back.shape

    def columns(step, carry):
        span = pl.ds(pl.multiple_of(step * TILE, TILE), TILE)
        out = back[:, :, span].reshape(dests * cap, TILE).astype(F32)
        weighted = (slot_gate[:, :1] * out).astype(BF16)
        spread_blocks(blocks, dot(pick[...], weighted, 0, 0).astype(BF16), span)
        return carry

    lax.fori_loop(0, width // TILE, columns, 0)


def combine_cot_kernel(top, back, pick, slot_gate, slot_place, *blocks):
    dests, cap, wide = back.shape
    width = wide - LANES
    count = dests * cap
    gate = slot_gate[:, :1]

    def columns(step, carry):
        span = pl.ds(pl.multiple_of(step * TILE, TILE), TILE)
        dx = back[:, :, span].reshape(count, TILE)
        spread_blocks(blocks, dot(pick[...], dx, 0, 0).astype(BF16), span)
        return carry

    lax.fori_loop(0, width // TILE, columns, 0)
    tail = back[:, :, width:].reshape(count, LANES).astype(F32)
    total = jnp.sum(tail, 1, keepdims=True) / jnp.where(gate > 0, gate, 1.0)
    lane = lax.broadcasted_iota(jnp.int32, (count, LANES), 1).astype(F32)
    spread = jnp.zeros((count, LANES), F32)
    for index, part in enumerate(split3(total)):
        spread = jnp.where(lane == slot_place[...] + float(index * top), part.astype(F32), spread)
    tail = dot(pick[...], spread.astype(BF16), 0, 0).astype(BF16)
    spread_blocks(blocks, tail, slice(width, wide))


def along(value, sign):
    size = lax.axis_size("z")
    pairs = []
    for z in range(size):
        pairs.append((2 * z, 2 * ((z + sign) % size)))
        pairs.append((2 * z + 1, 2 * ((z - sign) % size) + 1))
    return lax.ppermute(value, ("z", "c"), pairs)


def swap(value):
    return lax.ppermute(value, "c", [(0, 1), (1, 0)])


def ring_gather(block, pair):
    far = lax.axis_size("z") // 2
    blocks = [block]
    moving = pair
    for step in range(far):
        moving = along(moving if step < far - 1 else moving[: block.shape[0]], 1)
        blocks.append(moving)
    return blocks


def ring_reduce(blocks):
    rows = blocks[0].shape[0]
    far = len(blocks) - 1
    arrived = [along(blocks[step], -step).astype(F32) for step in range(1, far + 1)]
    both = sum(arrived[:-1])
    other = swap(both[rows:].astype(BF16))
    return blocks[0].astype(F32) + both[:rows] + arrived[-1] + other.astype(F32)


def merge_kernel(first_0, relayed_0, second_0, first_1, relayed_1, second_1, joined_0, joined_1):
    rows = first_0.shape[0]
    joined_0[:rows, :] = (first_0[...].astype(F32) + relayed_0[...].astype(F32)).astype(BF16)
    joined_0[rows:, :] = second_0[...]
    joined_1[:rows, :] = (first_1[...].astype(F32) + relayed_1[...].astype(F32)).astype(BF16)
    joined_1[rows:, :] = second_1[...]


def touch_kernel(left, right, left_out, right_out):
    del left, right, left_out, right_out


def touch(left, right, name):
    return pl.pallas_call(
        touch_kernel,
        out_shape=[jax.ShapeDtypeStruct(v.shape, v.dtype) for v in (left, right)],
        in_specs=[ANY] * 2,
        out_specs=[ANY] * 2,
        input_output_aliases={0: 0, 1: 1},
        cost_estimate=pl.CostEstimate(
            flops=COST[name] * 10**9, bytes_accessed=0, transcendentals=0
        ),
        name=name,
    )(left, right)


def final_kernel(own_0, own_1, before, after, gate_up_grad, down_grad):
    rows = own_0.shape[0]
    half = rows // 3
    for side, own in ((0, own_0), (1, own_1)):
        units = slice(side * half, (side + 1) * half)
        for kind in range(3):
            span = slice(kind * half, (kind + 1) * half)
            up = slice(side * rows + kind * half, side * rows + (kind + 1) * half)
            down = slice((1 - side) * rows + kind * half, (1 - side) * rows + (kind + 1) * half)
            total = own[span, :].astype(F32) + before[up, :].astype(F32)
            total = total + after[down, :].astype(F32)
            if kind < 2:
                gate_up_grad[0, units, kind, :] = total
            else:
                down_grad[0, units, :] = total


def body(tokens, expert_ids, route_gates, gate_up, down_weight, out_grad):
    tok_count, width = tokens.shape
    top = expert_ids.shape[1]
    z_size = lax.axis_size("z")
    dests = lax.axis_size("x") * 2
    cap = 6 * z_size
    count = dests * cap
    held = tok_count * z_size
    units = gate_up.shape[1]
    half = units // 2
    wide = width + LANES
    n = 8
    full = n * half

    double = 2 * width + LANES
    (packed,) = call(
        pack_kernel, [((tok_count, double), BF16)], [VMEM] * 4, [VMEM], [], 0, 0, MIB, "pack"
    )(tokens, expert_ids.T, route_gates.T, out_grad)
    pair = jnp.concatenate([packed, swap(packed)], 0)
    pair, gate_up, down_weight = lax.optimization_barrier((pair, gate_up, down_weight))
    blocks = ring_gather(packed, pair)
    three = 3 * half
    (own,) = call(
        weights_kernel,
        [((2 * three, width), BF16)],
        [VMEM] * 2,
        [VMEM],
        [],
        0,
        0,
        MIB,
        "weights",
    )(gate_up, down_weight)
    before = shift(own, "dp", 1)
    after = shift(own, "dp", -1)
    z_index = lax.axis_index("z").astype(jnp.int32).reshape(1)
    rows_type = ((dests, cap, width), BF16)
    pick_flops = 2 * count * held * width
    send, pick, slot_gate, slot_place = call(
        functools.partial(select_kernel, top, dests, cap),
        [((dests, 2 * cap, width), BF16), ((count, held), BF16)] + [((count, LANES), F32)] * 2,
        [SMEM] + [VMEM] * len(blocks),
        [VMEM] * 4,
        [pltpu.VMEM((held, double), BF16)],
        pick_flops,
        3 * 10**6,
        MIB,
        "select",
    )(z_index, *blocks)
    before, after, _ = lax.optimization_barrier((before, after, send))
    far_0 = shift(before[:three], "dp", 1)
    far_1 = shift(after[three:], "dp", -1)
    far_0, far_1 = touch(far_0, far_1, "touch")
    pieces = [own, before, after, far_0, far_1]

    arrived = lax.all_to_all(send, ("x", "c"), 0, 0, tiled=True)

    shards = n // 2 - 1
    hidden_type = ((count, units), BF16)
    piece_type = ((3 * half, width), BF16)
    weight = pltpu.VMEM((full, width), BF16)
    gate_all, up_all, hid, result, gcot_f, ucot_f, score_f, far_g0, far_g1 = call(
        forward_kernel,
        [((shards, count, units), F32)] * 2
        + [((shards, count, units), BF16), rows_type, hidden_type, hidden_type]
        + [((count, LANES), F32)]
        + [piece_type] * 2,
        [VMEM] + [ANY] * len(pieces),
        [VMEM] * 9,
        [pltpu.VMEM((count, units), BF16), pltpu.VMEM((3, units, count), BF16)]
        + [weight] * 3
        + [pltpu.SemaphoreType.DMA((3 * n,))],
        1,
        0,
        MIB,
        "forward",
    )(arrived, *pieces)
    result_cot, own_0, own_1, before_g0, before_g1, after_g0, after_g1 = call(
        backward_kernel,
        [((dests, cap, wide), BF16)] + [piece_type] * (n - 2),
        [VMEM] * 7 + [ANY] * len(pieces),
        [VMEM] * (n - 1),
        [pltpu.VMEM((shards, count, units), BF16)] * 2
        + [pltpu.VMEM((3, units * shards, count), BF16)]
        + [weight] * 3
        + [pltpu.SemaphoreType.DMA((3 * n - 2,))],
        1,
        0,
        MIB,
        "backward",
    )(arrived, gate_all, up_all, hid, gcot_f, ucot_f, score_f, *pieces)

    relay_0 = shift(far_g0, "dp", 1)
    relay_1 = shift(far_g1, "dp", -1)

    joined_0, joined_1 = call(
        merge_kernel,
        [((2 * three, width), BF16)] * 2,
        [VMEM] * 6,
        [VMEM] * 2,
        [],
        1,
        0,
        MIB,
        "merge",
    )(after_g0, relay_0, after_g1, before_g1, relay_1, before_g0)
    got_before = shift(joined_0, "dp", 1)
    got_after = shift(joined_1, "dp", -1)
    got_before, got_after = touch(got_before, got_after, "touch2")
    gate_up_grad, down_grad = call(
        final_kernel,
        [(gate_up.shape, F32), (down_weight.shape, F32)],
        [VMEM] * 4,
        [VMEM] * 2,
        [],
        0,
        0,
        MIB,
        "final",
    )(own_0, own_1, got_before, got_after)

    back = lax.all_to_all(result, ("x", "c"), 0, 0, tiled=True)
    parts = call(
        combine_kernel,
        [((b.shape[0], width), BF16) for b in blocks],
        [VMEM] * 3 + [ANY],
        [VMEM] * len(blocks),
        [],
        pick_flops,
        3 * 10**6,
        MIB,
        "combine",
    )(back, pick, slot_gate, joined_0)
    moe_out = ring_reduce(list(parts)).astype(BF16)
    back_cot = lax.all_to_all(result_cot, ("x", "c"), 0, 0, tiled=True)
    parts = call(
        functools.partial(combine_cot_kernel, top),
        [((b.shape[0], wide), BF16) for b in blocks],
        [VMEM] * 4,
        [VMEM] * len(blocks),
        [],
        pick_flops,
        3 * 10**6,
        MIB,
        "combine_cot",
    )(back_cot, pick, slot_gate, slot_place)
    summed = ring_reduce(list(parts))
    token_grad = summed[:, :width].astype(BF16)
    tail = summed[:, width:]
    gate_grad = tail[:, :top] + tail[:, top : 2 * top] + tail[:, 2 * top : 3 * top]
    return moe_out, gate_grad, token_grad, gate_up_grad, down_grad


def solution(mesh):
    wide = Mesh(mesh.devices.reshape(4, 4, 8, 2), ("dp", "x", "z", "c"))
    expert = ("x", "z", "c")
    every = ("dp",) + expert
    in_specs = (
        P(every, None),
        P(every, None),
        P(every, None),
        P(expert, "dp", None, None),
        P(expert, "dp", None),
        P(every, None),
    )
    out_specs = (
        P(every, None),
        P(every, None),
        P(every, None),
        P(expert, "dp", None, None),
        P(expert, "dp", None),
    )
    return jax.shard_map(body, mesh=wide, in_specs=in_specs, out_specs=out_specs, check_vma=False)
```

```python
import functools

import jax
import jax.numpy as jnp
from jax import lax
from jax.experimental import pallas as pl
from jax.experimental.pallas import tpu as pltpu
from jax.sharding import Mesh
from jax.sharding import PartitionSpec as P

F32 = jnp.float32
BF16 = jnp.bfloat16
LANES = 128
TILE = 1024
PIECES = 5
PLACES = ((0, 0), (0, 3), (1, 0), (1, 3), (2, 0), (2, 3), (3, 0), (4, 0))
MIB = 56
COST = {"pack": 0, "touch2": 0, "weights": 10, "select": 0, "merge": 80, "combine": 0, "combine_cot": 0, "forward": 1, "backward": 1, "final": 0, "touch": 10}
VMEM = pl.BlockSpec(memory_space=pltpu.VMEM)
SMEM = pl.BlockSpec(memory_space=pltpu.SMEM)
ANY = pl.BlockSpec(memory_space=pl.ANY)


def shift(value, axis, step):
    size = lax.axis_size(axis)
    return lax.ppermute(value, axis, [(i, (i + step) % size) for i in range(size)])


def dot(left, right, left_dim, right_dim):
    return lax.dot_general(
        left, right, (((left_dim,), (right_dim,)), ((), ())), preferred_element_type=F32
    )


def call(kernel, outs, in_specs, out_specs, scratch, flops, bytes_accessed, mib, name, grid=()):
    return pl.pallas_call(
        kernel,
        grid=grid,
        out_shape=[jax.ShapeDtypeStruct(s, d) for s, d in outs],
        in_specs=in_specs,
        out_specs=out_specs,
        scratch_shapes=scratch,
        compiler_params=pltpu.CompilerParams(vmem_limit_bytes=mib * 1024 * 1024),
        cost_estimate=pl.CostEstimate(
            flops=COST[name] * 10**9, bytes_accessed=0, transcendentals=0
        ),
        name=name,
    )


def strips(shape):
    lead = len(shape) - 1
    return pl.BlockSpec(tuple(shape[:-1]) + (TILE,), lambda step: (0,) * lead + (step,))


def split3(value):
    high = value.astype(BF16)
    rest = value - high.astype(F32)
    middle = rest.astype(BF16)
    low = (rest - middle.astype(F32)).astype(BF16)
    return high, middle, low


def pack_kernel(tokens, ids, gates, grads, packed):
    width = tokens.shape[1]
    top = ids.shape[0]
    row = lax.broadcasted_iota(jnp.int32, (top, LANES), 0)
    lane = lax.broadcasted_iota(jnp.int32, (top, LANES), 1)
    fields = (ids[...].astype(F32).astype(BF16),) + split3(gates[...])
    tail = jnp.zeros((tokens.shape[0], LANES), F32)
    for index, field in enumerate(fields):
        place = (lane == row + index * top).astype(F32).astype(BF16)
        tail = tail + dot(field, place, 0, 0)
    packed[:, :width] = tokens[...]
    packed[:, width : width + LANES] = tail.astype(BF16)
    packed[:, width + LANES :] = grads[...]


def weights_kernel(gate_up, down, own):
    half = own.shape[0] // 6
    for part in range(2):
        units = slice(part * half, (part + 1) * half)
        first = 3 * part * half
        for kind in range(2):
            rows = slice(first + kind * half, first + (kind + 1) * half)
            own[rows, :] = gate_up[0, units, kind, :]
        own[first + 2 * half : first + 3 * half, :] = down[0, units, :]


def gather_blocks(blocks, held):
    first = 0
    for block in blocks:
        held[first : first + block.shape[0], :] = block[...]
        first += block.shape[0]


def select_kernel(top, dests, cap, z_index, *refs):
    blocks = refs[:5]
    send, pick_out, gate_out, place_out, held = refs[-5:]
    width = send.shape[2]
    count = held.shape[0]
    gather_blocks(blocks, held)
    info = held[:, width : width + LANES].astype(F32).T
    ids = info[:top]
    gates = info[top : 2 * top] + info[2 * top : 3 * top] + info[3 * top : 4 * top]
    order = lax.broadcasted_iota(jnp.int32, (top, count), 0).astype(F32)
    base = (z_index[0] * 2).astype(F32)
    marks, gate_rows, place_rows = [], [], []
    for dest in range(dests):
        expert = base + float((dest // 2) * 16 + dest % 2)
        chosen = ids == expert
        marks.append(jnp.sum(jnp.where(chosen, 1.0, 0.0), 0, keepdims=True))
        gate_rows.append(jnp.sum(jnp.where(chosen, gates, 0.0), 0, keepdims=True))
        place_rows.append(jnp.sum(jnp.where(chosen, order, 0.0), 0, keepdims=True))
    mark = jnp.concatenate(marks, 0)
    before = lax.broadcasted_iota(jnp.int32, (count, count), 0) < lax.broadcasted_iota(
        jnp.int32, (count, count), 1
    )
    rank = dot(mark.astype(BF16), before.astype(F32).astype(BF16), 1, 0)
    rank = jnp.where(mark > 0, rank, -1.0)
    slot = lax.broadcasted_iota(jnp.int32, (cap, count), 0).astype(F32)
    slot_gates = []
    for dest in range(dests):
        span = slice(dest * cap, (dest + 1) * cap)
        hit = rank[dest : dest + 1] == slot
        pick_out[span, :] = jnp.where(hit, 1.0, 0.0).astype(BF16)
        slot_gate = jnp.sum(jnp.where(hit, gate_rows[dest], 0.0), 1, keepdims=True)
        slot_place = jnp.sum(jnp.where(hit, place_rows[dest], 0.0), 1, keepdims=True)
        gate_out[span, :] = jnp.broadcast_to(slot_gate, (cap, LANES))
        place_out[span, :] = jnp.broadcast_to(slot_place, (cap, LANES))
        slot_gates.append(slot_gate)
    slot_gate = jnp.concatenate(slot_gates, 0)

    def columns(step, carry):
        span = pl.ds(pl.multiple_of(step * TILE, TILE), TILE)
        tok = dot(pick_out[...], held[:, span], 1, 0).astype(BF16)
        send[:, :cap, span] = tok.reshape(dests, cap, TILE)
        second = pl.ds(pl.multiple_of(step * TILE + width + LANES, LANES), TILE)
        cot = slot_gate * dot(pick_out[...], held[:, second], 1, 0)
        send[:, cap:, span] = cot.astype(BF16).reshape(dests, cap, TILE)
        return carry

    lax.fori_loop(0, width // TILE, columns, 0)


def load(pieces, places, weights, sems, skip=0):
    half = pieces[-1].shape[0] // 3
    copies = []
    for index, (number, first) in enumerate(places):
        group = []
        for slot, (kind, weight) in enumerate(weights):
            copy = pltpu.make_async_copy(
                pieces[number].at[pl.ds(first * half + kind * half, half), :],
                weight.at[pl.ds((index + skip) * half, half), :],
                sems.at[index * len(weights) + slot],
            )
            copy.start()
            group.append(copy)
        copies.append(group)
    return copies


def wait_all(copies):
    for group in copies:
        for copy in group:
            copy.wait()


def hidden_parts(gate_pre, up_pre, hidden_cot):
    sigma = jax.nn.sigmoid(gate_pre)
    gate_cot = hidden_cot * up_pre * sigma * (1.0 + gate_pre * (1.0 - sigma))
    return gate_cot, hidden_cot * (gate_pre * sigma)


def fold(value):
    wide = jnp.concatenate([value, jnp.zeros((value.shape[0], 64), F32)], 1)
    return wide[:, :LANES] + wide[:, LANES:]


def forward_kernel(arrived_hbm, *refs):
    pieces = refs[:PIECES]
    outs = refs[PIECES : PIECES + 6]
    gcot, ucot, score = refs[PIECES + 6 : PIECES + 9]
    held = refs[PIECES + 9 : PIECES + 15]
    gate_all, up_all, hid, result, grad_0, grad_1 = held
    arrived, hid_far, lefts, w_gate, w_up, w_down, sems, in_sems, out_sems = refs[PIECES + 15 :]
    dests, double, width = arrived.shape
    cap = double // 2
    count = dests * cap
    half = grad_0.shape[0] // 3
    shards = len(PLACES) // 2
    kinds = ((0, w_gate), (1, w_up), (2, w_down))
    arrival = pltpu.make_async_copy(arrived_hbm, arrived, in_sems.at[0])
    arrival.start()
    copies = load(pieces, PLACES[-2:], kinds, sems.at[pl.ds(0, 6)])
    arrival.wait()
    wait_all(copies)
    near = len(PLACES) - 2
    copies = load(pieces, PLACES[:-2], kinds, sems.at[pl.ds(6, 3 * near)], 2)
    rows = arrived[:, :cap, :].reshape(count, width)
    leaving = []

    def leave(index):
        copy = pltpu.make_async_copy(held[index], outs[index], out_sems.at[index])
        copy.start()
        leaving.append(copy)

    hidden = []
    for shard in range(shards):
        if shard:
            wait_all(copies[2 * shard - 2 : 2 * shard])
        span = slice(2 * shard * half, 2 * (shard + 1) * half)
        gate_pre = dot(rows, w_gate[span, :], 1, 1)
        up_pre = dot(rows, w_up[span, :], 1, 1)
        value = (gate_pre * jax.nn.sigmoid(gate_pre) * up_pre).astype(BF16)
        if shard:
            gate_all[shard - 1], up_all[shard - 1], hid[shard - 1] = gate_pre, up_pre, value
            hidden.append(hid.at[shard - 1])
            continue
        hid_far[...] = value
        hidden.append(hid_far)
        hidden_cot = dot(arrived[:, cap:, :].reshape(count, width), w_down[span, :], 1, 1)
        gate_cot, up_cot = hidden_parts(gate_pre, up_pre, hidden_cot)
        gcot[...] = gate_cot.astype(BF16)
        ucot[...] = up_cot.astype(BF16)
        score[...] = fold(value.astype(F32) * hidden_cot)
        lefts[0] = gate_cot.T.astype(BF16)
        lefts[1] = up_cot.T.astype(BF16)
        lefts[2] = value.astype(F32).T.astype(BF16)
        write_grads(arrived, lefts, (grad_0, grad_1))
        leave(4)
        leave(5)
    for index in range(3):
        leave(index)

    def columns(step, carry):
        span = pl.ds(pl.multiple_of(step * TILE, TILE), TILE)
        out = jnp.zeros((count, TILE), F32)
        for shard, value in enumerate(hidden):
            units = slice(2 * shard * half, 2 * (shard + 1) * half)
            out = out + dot(value[...], w_down[units, span], 1, 0)
        result[:, :, span] = out.astype(BF16).reshape(dests, cap, TILE)
        return carry

    lax.fori_loop(0, width // TILE, columns, 0)
    leave(3)
    for copy in leaving:
        copy.wait()


def write_grads(arrived, lefts, pieces):
    dests, double, width = arrived.shape
    cap = double // 2
    count = dests * cap
    half = pieces[0].shape[0] // 3

    def columns(step, carry):
        span = pl.ds(pl.multiple_of(step * TILE, TILE), TILE)
        rows = arrived[:, :cap, span].reshape(count, TILE)
        cots = arrived[:, cap:, span].reshape(count, TILE)
        for kind, right in enumerate((rows, rows, cots)):
            grad = dot(lefts[kind], right, 1, 0).astype(BF16)
            for index, piece in enumerate(pieces):
                piece[kind * half : (kind + 1) * half, span] = grad[
                    index * half : (index + 1) * half
                ]
        return carry

    lax.fori_loop(0, width // TILE, columns, 0)


def backward_kernel(arrived, gate_all, up_all, hid, gcot_far, ucot_far, score_far, *refs):
    pieces = refs[:PIECES]
    near = len(PLACES) - 2
    result = refs[PIECES]
    grads = refs[PIECES + 1 : PIECES + 1 + near]
    gcot, ucot, lefts, w_gate, w_up, w_down, sems = refs[PIECES + 1 + near :]
    dests, double, width = arrived.shape
    cap = double // 2
    count = dests * cap
    half = grads[0].shape[0] // 3
    copies = load(pieces, PLACES[:near], ((2, w_down),), sems.at[pl.ds(0, near)])
    others = load(pieces, PLACES, ((0, w_gate), (1, w_up)), sems.at[pl.ds(near, 2 * near + 4)])
    cots = arrived[:, cap:, :].reshape(count, width)
    score = score_far[...]
    for shard in range(near // 2):
        wait_all(copies[2 * shard : 2 * shard + 2])
        span = slice(2 * shard * half, 2 * (shard + 1) * half)
        hidden_cot = dot(cots, w_down[span, :], 1, 1)
        hidden = hid[shard].astype(F32)
        gate_cot, up_cot = hidden_parts(gate_all[shard], up_all[shard], hidden_cot)
        gcot[shard] = gate_cot.astype(BF16)
        ucot[shard] = up_cot.astype(BF16)
        lefts[0, span, :] = gate_cot.T.astype(BF16)
        lefts[1, span, :] = up_cot.T.astype(BF16)
        lefts[2, span, :] = hidden.T.astype(BF16)
        score = score + fold(hidden * hidden_cot)
    total = jnp.sum(score, 1, keepdims=True)
    lane = lax.broadcasted_iota(jnp.int32, (count, LANES), 1)
    high, middle, low = (part.astype(F32) for part in split3(total))
    tail = jnp.where(lane == 0, high, jnp.where(lane == 1, middle, jnp.where(lane == 2, low, 0.0)))
    result[:, :, width:] = tail.astype(BF16).reshape(dests, cap, LANES)
    write_grads(arrived, lefts, grads)
    wait_all(others)

    def columns(step, carry):
        span = pl.ds(pl.multiple_of(step * TILE, TILE), TILE)
        first = half * near
        dx = dot(gcot_far[...], w_gate[first:, span], 1, 0)
        dx = dx + dot(ucot_far[...], w_up[first:, span], 1, 0)
        for shard in range(near // 2):
            units = slice(2 * shard * half, 2 * (shard + 1) * half)
            dx = dx + dot(gcot[shard], w_gate[units, span], 1, 0)
            dx = dx + dot(ucot[shard], w_up[units, span], 1, 0)
        result[:, :, span] = dx.astype(BF16).reshape(dests, cap, TILE)
        return carry

    lax.fori_loop(0, width // TILE, columns, 0)


def spread_blocks(blocks, value, span):
    first = 0
    for block in blocks:
        block[:, span] = value[first : first + block.shape[0]]
        first += block.shape[0]


def combine_kernel(back, pick, slot_gate, joined, *blocks):
    del joined
    dests, cap, width = back.shape

    def columns(step, carry):
        span = pl.ds(pl.multiple_of(step * TILE, TILE), TILE)
        out = back[:, :, span].reshape(dests * cap, TILE).astype(F32)
        weighted = (slot_gate[:, :1] * out).astype(BF16)
        spread_blocks(blocks, dot(pick[...], weighted, 0, 0).astype(BF16), span)
        return carry

    lax.fori_loop(0, width // TILE, columns, 0)


def combine_cot_kernel(top, back, pick, slot_gate, slot_place, *blocks):
    dests, cap, wide = back.shape
    width = wide - LANES
    count = dests * cap
    gate = slot_gate[:, :1]

    def columns(step, carry):
        span = pl.ds(pl.multiple_of(step * TILE, TILE), TILE)
        dx = back[:, :, span].reshape(count, TILE)
        spread_blocks(blocks, dot(pick[...], dx, 0, 0).astype(BF16), span)
        return carry

    lax.fori_loop(0, width // TILE, columns, 0)
    tail = back[:, :, width:].reshape(count, LANES).astype(F32)
    total = jnp.sum(tail, 1, keepdims=True) / jnp.where(gate > 0, gate, 1.0)
    lane = lax.broadcasted_iota(jnp.int32, (count, LANES), 1).astype(F32)
    spread = jnp.zeros((count, LANES), F32)
    for index, part in enumerate(split3(total)):
        spread = jnp.where(lane == slot_place[...] + float(index * top), part.astype(F32), spread)
    tail = dot(pick[...], spread.astype(BF16), 0, 0).astype(BF16)
    spread_blocks(blocks, tail, slice(width, wide))


def along(value, sign):
    size = lax.axis_size("z")
    pairs = []
    for z in range(size):
        pairs.append((2 * z, 2 * ((z + sign) % size)))
        pairs.append((2 * z + 1, 2 * ((z - sign) % size) + 1))
    return lax.ppermute(value, ("z", "c"), pairs)


def swap(value):
    return lax.ppermute(value, "c", [(0, 1), (1, 0)])


def ring_gather(block, pair):
    far = lax.axis_size("z") // 2
    blocks = [block]
    moving = pair
    for step in range(far):
        moving = along(moving if step < far - 1 else moving[: block.shape[0]], 1)
        blocks.append(moving)
    return blocks


def add(left, right):
    return (left.astype(F32) + right.astype(F32)).astype(BF16)


def ring_reduce(blocks, after=None):
    rows = blocks[0].shape[0]
    far = len(blocks) - 1
    hop = along(blocks[far], -1)
    arrived = [along(blocks[step], -step) for step in range(1, far - 1)]
    last = add(blocks[far - 1], jnp.pad(hop, ((0, rows), (0, 0))))
    arrived.append(along(last, 1 - far))
    if after is not None:
        *arrived, _ = lax.optimization_barrier((*arrived, after))
    both = sum(value.astype(F32) for value in arrived)
    other = swap(both[rows:].astype(BF16))
    return blocks[0].astype(F32) + both[:rows] + other.astype(F32)


def merge_kernel(first_0, relayed_0, second_0, first_1, relayed_1, second_1, joined_0, joined_1):
    rows = first_0.shape[0]
    joined_0[:rows, :] = (first_0[...].astype(F32) + relayed_0[...].astype(F32)).astype(BF16)
    joined_0[rows:, :] = second_0[...]
    joined_1[:rows, :] = (first_1[...].astype(F32) + relayed_1[...].astype(F32)).astype(BF16)
    joined_1[rows:, :] = second_1[...]


def touch_kernel(left, right, left_out, right_out):
    del left, right, left_out, right_out


def touch(left, right, name):
    return pl.pallas_call(
        touch_kernel,
        out_shape=[jax.ShapeDtypeStruct(v.shape, v.dtype) for v in (left, right)],
        in_specs=[ANY] * 2,
        out_specs=[ANY] * 2,
        input_output_aliases={0: 0, 1: 1},
        cost_estimate=pl.CostEstimate(
            flops=COST[name] * 10**9, bytes_accessed=0, transcendentals=0
        ),
        name=name,
    )(left, right)


def final_kernel(own_0, own_1, before, after, gate_up_grad, down_grad):
    rows = own_0.shape[0]
    half = rows // 3
    for side, own in ((0, own_0), (1, own_1)):
        units = slice(side * half, (side + 1) * half)
        for kind in range(3):
            span = slice(kind * half, (kind + 1) * half)
            up = slice(side * rows + kind * half, side * rows + (kind + 1) * half)
            down = slice((1 - side) * rows + kind * half, (1 - side) * rows + (kind + 1) * half)
            total = own[span, :].astype(F32) + before[up, :].astype(F32)
            total = total + after[down, :].astype(F32)
            if kind < 2:
                gate_up_grad[0, units, kind, :] = total
            else:
                down_grad[0, units, :] = total


def body(tokens, expert_ids, route_gates, gate_up, down_weight, out_grad):
    tok_count, width = tokens.shape
    top = expert_ids.shape[1]
    z_size = lax.axis_size("z")
    dests = lax.axis_size("x") * 2
    cap = 6 * z_size
    count = dests * cap
    held = tok_count * z_size
    units = gate_up.shape[1]
    half = units // 2
    wide = width + LANES
    n = 8
    full = n * half

    double = 2 * width + LANES
    (packed,) = call(
        pack_kernel, [((tok_count, double), BF16)], [VMEM] * 4, [VMEM], [], 0, 0, MIB, "pack"
    )(tokens, expert_ids.T, route_gates.T, out_grad)
    pair = jnp.concatenate([packed, swap(packed)], 0)
    pair, gate_up, down_weight = lax.optimization_barrier((pair, gate_up, down_weight))
    blocks = ring_gather(packed, pair)
    three = 3 * half
    (own,) = call(
        weights_kernel,
        [((2 * three, width), BF16)],
        [strips(gate_up.shape), strips(down_weight.shape)],
        [strips((2 * three, width))],
        [],
        0,
        0,
        MIB,
        "weights",
        (width // TILE,),
    )(gate_up, down_weight)
    before = shift(own, "dp", 1)
    after = shift(own, "dp", -1)
    z_index = lax.axis_index("z").astype(jnp.int32).reshape(1)
    rows_type = ((dests, cap, width), BF16)
    pick_flops = 2 * count * held * width
    send, pick, slot_gate, slot_place = call(
        functools.partial(select_kernel, top, dests, cap),
        [((dests, 2 * cap, width), BF16), ((count, held), BF16)] + [((count, LANES), F32)] * 2,
        [SMEM] + [VMEM] * len(blocks),
        [VMEM] * 4,
        [pltpu.VMEM((held, double), BF16)],
        pick_flops,
        3 * 10**6,
        MIB,
        "select",
    )(z_index, *blocks)
    before, _ = lax.optimization_barrier((before, send))
    after, _ = lax.optimization_barrier((after, send))
    far_0 = shift(before[:three], "dp", 1)
    far_1 = shift(after[three:], "dp", -1)
    far_0, far_1 = touch(far_0, far_1, "touch")
    pieces = [own, before, after, far_0, far_1]

    arrived = lax.all_to_all(send, ("x", "c"), 0, 0, tiled=True)

    shards = n // 2 - 1
    hidden_type = ((count, units), BF16)
    piece_type = ((3 * half, width), BF16)
    weight = pltpu.VMEM((full, width), BF16)
    held_types = [((shards, count, units), F32)] * 2 + [((shards, count, units), BF16), rows_type]
    held_types = held_types + [piece_type] * 2
    gate_all, up_all, hid, result, far_g0, far_g1, gcot_f, ucot_f, score_f = call(
        forward_kernel,
        held_types + [hidden_type, hidden_type, ((count, LANES), F32)],
        [ANY] * (1 + len(pieces)),
        [ANY] * 6 + [VMEM] * 3,
        [pltpu.VMEM(s, d) for s, d in held_types]
        + [pltpu.VMEM((dests, 2 * cap, width), BF16)]
        + [pltpu.VMEM((count, units), BF16), pltpu.VMEM((3, units, count), BF16)]
        + [weight] * 3
        + [pltpu.SemaphoreType.DMA((k,)) for k in (3 * n, 1, 6)],
        1,
        0,
        MIB,
        "forward",
    )(arrived, *pieces)
    result_cot, own_0, own_1, before_g0, before_g1, after_g0, after_g1 = call(
        backward_kernel,
        [((dests, cap, wide), BF16)] + [piece_type] * (n - 2),
        [VMEM] * 7 + [ANY] * len(pieces),
        [VMEM] * (n - 1),
        [pltpu.VMEM((shards, count, units), BF16)] * 2
        + [pltpu.VMEM((3, units * shards, count), BF16)]
        + [weight] * 3
        + [pltpu.SemaphoreType.DMA((3 * n - 2,))],
        1,
        0,
        MIB,
        "backward",
    )(arrived, gate_all, up_all, hid, gcot_f, ucot_f, score_f, *pieces)

    relay_0 = shift(far_g0, "dp", 1)
    relay_1 = shift(far_g1, "dp", -1)

    joined_0, joined_1 = call(
        merge_kernel,
        [((2 * three, width), BF16)] * 2,
        [strips((three, width))] * 6,
        [strips((2 * three, width))] * 2,
        [],
        1,
        0,
        MIB,
        "merge",
        (width // TILE,),
    )(after_g0, relay_0, after_g1, before_g1, relay_1, before_g0)
    got_before = shift(joined_0, "dp", 1)
    got_after = shift(joined_1, "dp", -1)
    got_before, got_after = touch(got_before, got_after, "touch2")
    gate_up_grad, down_grad = call(
        final_kernel,
        [(gate_up.shape, F32), (down_weight.shape, F32)],
        [strips((three, width))] * 2 + [strips((2 * three, width))] * 2,
        [strips(gate_up.shape), strips(down_weight.shape)],
        [],
        0,
        0,
        MIB,
        "final",
        (width // TILE,),
    )(own_0, own_1, got_before, got_after)

    back = lax.all_to_all(result, ("x", "c"), 0, 0, tiled=True)
    parts = call(
        combine_kernel,
        [((b.shape[0], width), BF16) for b in blocks],
        [VMEM] * 3 + [ANY],
        [VMEM] * len(blocks),
        [],
        pick_flops,
        3 * 10**6,
        MIB,
        "combine",
    )(back, pick, slot_gate, joined_0)
    moe_out = ring_reduce(list(parts)).astype(BF16)
    back_cot = lax.all_to_all(result_cot, ("x", "c"), 0, 0, tiled=True)
    parts = call(
        functools.partial(combine_cot_kernel, top),
        [((b.shape[0], wide), BF16) for b in blocks],
        [VMEM] * 4,
        [VMEM] * len(blocks),
        [],
        pick_flops,
        3 * 10**6,
        MIB,
        "combine_cot",
    )(back_cot, pick, slot_gate, slot_place)
    summed = ring_reduce(list(parts), down_grad)
    token_grad = summed[:, :width].astype(BF16)
    tail = summed[:, width:]
    gate_grad = tail[:, :top] + tail[:, top : 2 * top] + tail[:, 2 * top : 3 * top]
    return moe_out, gate_grad, token_grad, gate_up_grad, down_grad


def solution(mesh):
    wide = Mesh(mesh.devices.reshape(4, 4, 8, 2), ("dp", "x", "z", "c"))
    expert = ("x", "z", "c")
    every = ("dp",) + expert
    in_specs = (
        P(every, None),
        P(every, None),
        P(every, None),
        P(expert, "dp", None, None),
        P(expert, "dp", None),
        P(every, None),
    )
    out_specs = (
        P(every, None),
        P(every, None),
        P(every, None),
        P(expert, "dp", None, None),
        P(expert, "dp", None),
    )
    return jax.shard_map(body, mesh=wide, in_specs=in_specs, out_specs=out_specs, check_vma=False)
```

```python
import functools

import jax
import jax.numpy as jnp
from jax import lax
from jax.experimental import pallas as pl
from jax.experimental.pallas import tpu as pltpu
from jax.sharding import Mesh
from jax.sharding import PartitionSpec as P

F32 = jnp.float32
BF16 = jnp.bfloat16
LANES = 128
TILE = 1024
WIDE = 2048
PIECES = 5
PLACES = ((0, 0), (0, 3), (1, 0), (1, 3), (2, 0), (2, 3), (3, 0), (4, 0))
MIB = 56
COST = {"pack": 0, "touch2": 0, "weights": 10, "select": 0, "merge": 80, "combine": 0, "combine_cot": 0, "forward": 1, "backward": 1, "final": 0, "touch": 10}
VMEM = pl.BlockSpec(memory_space=pltpu.VMEM)
SMEM = pl.BlockSpec(memory_space=pltpu.SMEM)
ANY = pl.BlockSpec(memory_space=pl.ANY)


def shift(value, axis, step):
    size = lax.axis_size(axis)
    return lax.ppermute(value, axis, [(i, (i + step) % size) for i in range(size)])


def dot(left, right, left_dim, right_dim):
    return lax.dot_general(
        left, right, (((left_dim,), (right_dim,)), ((), ())), preferred_element_type=F32
    )


def call(kernel, outs, in_specs, out_specs, scratch, flops, bytes_accessed, mib, name, grid=()):
    return pl.pallas_call(
        kernel,
        grid=grid,
        out_shape=[jax.ShapeDtypeStruct(s, d) for s, d in outs],
        in_specs=in_specs,
        out_specs=out_specs,
        scratch_shapes=scratch,
        compiler_params=pltpu.CompilerParams(vmem_limit_bytes=mib * 1024 * 1024),
        cost_estimate=pl.CostEstimate(
            flops=COST[name] * 10**9, bytes_accessed=0, transcendentals=0
        ),
        name=name,
    )


def strips(shape):
    lead = len(shape) - 1
    return pl.BlockSpec(tuple(shape[:-1]) + (TILE,), lambda step: (0,) * lead + (step,))


def split3(value):
    high = value.astype(BF16)
    rest = value - high.astype(F32)
    middle = rest.astype(BF16)
    low = (rest - middle.astype(F32)).astype(BF16)
    return high, middle, low


def pack_kernel(tokens, ids, gates, packed):
    width = tokens.shape[1]
    top = ids.shape[0]
    row = lax.broadcasted_iota(jnp.int32, (top, LANES), 0)
    lane = lax.broadcasted_iota(jnp.int32, (top, LANES), 1)
    fields = (ids[...].astype(F32).astype(BF16),) + split3(gates[...])
    tail = jnp.zeros((tokens.shape[0], LANES), F32)
    for index, field in enumerate(fields):
        place = (lane == row + index * top).astype(F32).astype(BF16)
        tail = tail + dot(field, place, 0, 0)
    packed[:, :width] = tokens[...]
    packed[:, width:] = tail.astype(BF16)


def weights_kernel(gate_up, down, own):
    half = own.shape[0] // 6
    for part in range(2):
        units = slice(part * half, (part + 1) * half)
        first = 3 * part * half
        for kind in range(2):
            rows = slice(first + kind * half, first + (kind + 1) * half)
            own[rows, :] = gate_up[0, units, kind, :]
        own[first + 2 * half : first + 3 * half, :] = down[0, units, :]


def gather_blocks(blocks, held):
    first = 0
    for block in blocks:
        held[first : first + block.shape[0], :] = block[...]
        first += block.shape[0]


def select_kernel(top, dests, cap, z_index, *refs):
    blocks, grad_blocks = refs[:5], refs[5:10]
    send, pick_out, gate_out, place_out, held, held_grads = refs[-6:]
    width = send.shape[2]
    count = held.shape[0]
    gather_blocks(blocks, held)
    gather_blocks(grad_blocks, held_grads)
    info = held[:, width:].astype(F32).T
    ids = info[:top]
    gates = info[top : 2 * top] + info[2 * top : 3 * top] + info[3 * top : 4 * top]
    order = lax.broadcasted_iota(jnp.int32, (top, count), 0).astype(F32)
    base = (z_index[0] * 2).astype(F32)
    marks, gate_rows, place_rows = [], [], []
    for dest in range(dests):
        expert = base + float((dest // 2) * 16 + dest % 2)
        chosen = ids == expert
        marks.append(jnp.sum(jnp.where(chosen, 1.0, 0.0), 0, keepdims=True))
        gate_rows.append(jnp.sum(jnp.where(chosen, gates, 0.0), 0, keepdims=True))
        place_rows.append(jnp.sum(jnp.where(chosen, order, 0.0), 0, keepdims=True))
    mark = jnp.concatenate(marks, 0)
    before = lax.broadcasted_iota(jnp.int32, (count, count), 0) < lax.broadcasted_iota(
        jnp.int32, (count, count), 1
    )
    rank = dot(mark.astype(BF16), before.astype(F32).astype(BF16), 1, 0)
    rank = jnp.where(mark > 0, rank, -1.0)
    slot = lax.broadcasted_iota(jnp.int32, (cap, count), 0).astype(F32)
    slot_gates = []
    for dest in range(dests):
        span = slice(dest * cap, (dest + 1) * cap)
        hit = rank[dest : dest + 1] == slot
        pick_out[span, :] = jnp.where(hit, 1.0, 0.0).astype(BF16)
        slot_gate = jnp.sum(jnp.where(hit, gate_rows[dest], 0.0), 1, keepdims=True)
        slot_place = jnp.sum(jnp.where(hit, place_rows[dest], 0.0), 1, keepdims=True)
        gate_out[span, :] = jnp.broadcast_to(slot_gate, (cap, LANES))
        place_out[span, :] = jnp.broadcast_to(slot_place, (cap, LANES))
        slot_gates.append(slot_gate)
    slot_gate = jnp.concatenate(slot_gates, 0)

    def columns(step, carry):
        span = pl.ds(pl.multiple_of(step * WIDE, WIDE), WIDE)
        tok = dot(pick_out[...], held[:, span], 1, 0).astype(BF16)
        send[:, :cap, span] = tok.reshape(dests, cap, WIDE)
        cot = slot_gate * dot(pick_out[...], held_grads[:, span], 1, 0)
        send[:, cap:, span] = cot.astype(BF16).reshape(dests, cap, WIDE)
        return carry

    lax.fori_loop(0, width // WIDE, columns, 0)


def load(pieces, places, weights, sems, skip=0):
    half = pieces[-1].shape[0] // 3
    copies = []
    for index, (number, first) in enumerate(places):
        group = []
        for slot, (kind, weight) in enumerate(weights):
            copy = pltpu.make_async_copy(
                pieces[number].at[pl.ds(first * half + kind * half, half), :],
                weight.at[pl.ds((index + skip) * half, half), :],
                sems.at[index * len(weights) + slot],
            )
            copy.start()
            group.append(copy)
        copies.append(group)
    return copies


def wait_all(copies):
    for group in copies:
        for copy in group:
            copy.wait()


def hidden_parts(gate_pre, up_pre, hidden_cot):
    sigma = jax.nn.sigmoid(gate_pre)
    gate_cot = hidden_cot * up_pre * sigma * (1.0 + gate_pre * (1.0 - sigma))
    return gate_cot, hidden_cot * (gate_pre * sigma)


def fold(value):
    wide = jnp.concatenate([value, jnp.zeros((value.shape[0], 64), F32)], 1)
    return wide[:, :LANES] + wide[:, LANES:]


def forward_kernel(arrived_hbm, *refs):
    pieces = refs[:PIECES]
    outs = refs[PIECES : PIECES + 6]
    gcot, ucot, score = refs[PIECES + 6 : PIECES + 9]
    held = refs[PIECES + 9 : PIECES + 15]
    gate_all, up_all, hid, result, grad_0, grad_1 = held
    arrived, hid_far, lefts, w_gate, w_up, w_down, sems, in_sems, out_sems = refs[PIECES + 15 :]
    dests, double, width = arrived.shape
    cap = double // 2
    count = dests * cap
    half = grad_0.shape[0] // 3
    shards = len(PLACES) // 2
    kinds = ((0, w_gate), (1, w_up), (2, w_down))
    arrival = pltpu.make_async_copy(arrived_hbm, arrived, in_sems.at[0])
    arrival.start()
    copies = load(pieces, PLACES[-2:], kinds, sems.at[pl.ds(0, 6)])
    arrival.wait()
    wait_all(copies)
    near = len(PLACES) - 2
    copies = load(pieces, PLACES[:-2], kinds, sems.at[pl.ds(6, 3 * near)], 2)
    rows = arrived[:, :cap, :].reshape(count, width)
    leaving = []

    def leave(index):
        copy = pltpu.make_async_copy(held[index], outs[index], out_sems.at[index])
        copy.start()
        leaving.append(copy)

    hidden = []
    for shard in range(shards):
        if shard:
            wait_all(copies[2 * shard - 2 : 2 * shard])
        span = slice(2 * shard * half, 2 * (shard + 1) * half)
        gate_pre = dot(rows, w_gate[span, :], 1, 1)
        up_pre = dot(rows, w_up[span, :], 1, 1)
        value = (gate_pre * jax.nn.sigmoid(gate_pre) * up_pre).astype(BF16)
        if shard:
            gate_all[shard - 1], up_all[shard - 1], hid[shard - 1] = gate_pre, up_pre, value
            hidden.append(hid.at[shard - 1])
            continue
        hid_far[...] = value
        hidden.append(hid_far)
        hidden_cot = dot(arrived[:, cap:, :].reshape(count, width), w_down[span, :], 1, 1)
        gate_cot, up_cot = hidden_parts(gate_pre, up_pre, hidden_cot)
        gcot[...] = gate_cot.astype(BF16)
        ucot[...] = up_cot.astype(BF16)
        score[...] = fold(value.astype(F32) * hidden_cot)
        lefts[0] = gate_cot.T.astype(BF16)
        lefts[1] = up_cot.T.astype(BF16)
        lefts[2] = value.astype(F32).T.astype(BF16)
        write_grads(arrived, lefts, (grad_0, grad_1))
        leave(4)
        leave(5)
    for index in range(3):
        leave(index)

    def columns(step, carry):
        span = pl.ds(pl.multiple_of(step * TILE, TILE), TILE)
        out = jnp.zeros((count, TILE), F32)
        for shard, value in enumerate(hidden):
            units = slice(2 * shard * half, 2 * (shard + 1) * half)
            out = out + dot(value[...], w_down[units, span], 1, 0)
        result[:, :, span] = out.astype(BF16).reshape(dests, cap, TILE)
        return carry

    lax.fori_loop(0, width // TILE, columns, 0)
    leave(3)
    for copy in leaving:
        copy.wait()


def write_grads(arrived, lefts, pieces):
    dests, double, width = arrived.shape
    cap = double // 2
    count = dests * cap
    half = pieces[0].shape[0] // 3

    def columns(step, carry):
        span = pl.ds(pl.multiple_of(step * TILE, TILE), TILE)
        rows = arrived[:, :cap, span].reshape(count, TILE)
        cots = arrived[:, cap:, span].reshape(count, TILE)
        for kind, right in enumerate((rows, rows, cots)):
            grad = dot(lefts[kind], right, 1, 0).astype(BF16)
            for index, piece in enumerate(pieces):
                piece[kind * half : (kind + 1) * half, span] = grad[
                    index * half : (index + 1) * half
                ]
        return carry

    lax.fori_loop(0, width // TILE, columns, 0)


def backward_kernel(arrived, gate_all, up_all, hid, gcot_far, ucot_far, score_far, *refs):
    pieces = refs[:PIECES]
    near = len(PLACES) - 2
    result = refs[PIECES]
    grads = refs[PIECES + 1 : PIECES + 1 + near]
    gcot, ucot, lefts, w_gate, w_up, w_down, sems = refs[PIECES + 1 + near :]
    dests, double, width = arrived.shape
    cap = double // 2
    count = dests * cap
    half = grads[0].shape[0] // 3
    copies = load(pieces, PLACES[:near], ((2, w_down),), sems.at[pl.ds(0, near)])
    others = load(pieces, PLACES, ((0, w_gate), (1, w_up)), sems.at[pl.ds(near, 2 * near + 4)])
    cots = arrived[:, cap:, :].reshape(count, width)
    score = score_far[...]
    for shard in range(near // 2):
        wait_all(copies[2 * shard : 2 * shard + 2])
        span = slice(2 * shard * half, 2 * (shard + 1) * half)
        hidden_cot = dot(cots, w_down[span, :], 1, 1)
        hidden = hid[shard].astype(F32)
        gate_cot, up_cot = hidden_parts(gate_all[shard], up_all[shard], hidden_cot)
        gcot[shard] = gate_cot.astype(BF16)
        ucot[shard] = up_cot.astype(BF16)
        lefts[0, span, :] = gate_cot.T.astype(BF16)
        lefts[1, span, :] = up_cot.T.astype(BF16)
        lefts[2, span, :] = hidden.T.astype(BF16)
        score = score + fold(hidden * hidden_cot)
    total = jnp.sum(score, 1, keepdims=True)
    lane = lax.broadcasted_iota(jnp.int32, (count, LANES), 1)
    high, middle, low = (part.astype(F32) for part in split3(total))
    tail = jnp.where(lane == 0, high, jnp.where(lane == 1, middle, jnp.where(lane == 2, low, 0.0)))
    result[:, :, width:] = tail.astype(BF16).reshape(dests, cap, LANES)
    write_grads(arrived, lefts, grads)
    wait_all(others)

    def columns(step, carry):
        span = pl.ds(pl.multiple_of(step * TILE, TILE), TILE)
        first = half * near
        dx = dot(gcot_far[...], w_gate[first:, span], 1, 0)
        dx = dx + dot(ucot_far[...], w_up[first:, span], 1, 0)
        for shard in range(near // 2):
            units = slice(2 * shard * half, 2 * (shard + 1) * half)
            dx = dx + dot(gcot[shard], w_gate[units, span], 1, 0)
            dx = dx + dot(ucot[shard], w_up[units, span], 1, 0)
        result[:, :, span] = dx.astype(BF16).reshape(dests, cap, TILE)
        return carry

    lax.fori_loop(0, width // TILE, columns, 0)


def spread_blocks(blocks, value, span):
    first = 0
    for block in blocks:
        block[:, span] = value[first : first + block.shape[0]]
        first += block.shape[0]


def combine_kernel(back, pick, slot_gate, joined, *blocks):
    del joined
    dests, cap, width = back.shape

    def columns(step, carry):
        span = pl.ds(pl.multiple_of(step * WIDE, WIDE), WIDE)
        out = back[:, :, span].reshape(dests * cap, WIDE).astype(F32)
        weighted = (slot_gate[:, :1] * out).astype(BF16)
        spread_blocks(blocks, dot(pick[...], weighted, 0, 0).astype(BF16), span)
        return carry

    lax.fori_loop(0, width // WIDE, columns, 0)


def combine_cot_kernel(top, back, pick, slot_gate, slot_place, *blocks):
    dests, cap, wide = back.shape
    width = wide - LANES
    count = dests * cap
    gate = slot_gate[:, :1]

    def columns(step, carry):
        span = pl.ds(pl.multiple_of(step * WIDE, WIDE), WIDE)
        dx = back[:, :, span].reshape(count, WIDE)
        spread_blocks(blocks, dot(pick[...], dx, 0, 0).astype(BF16), span)
        return carry

    lax.fori_loop(0, width // WIDE, columns, 0)
    tail = back[:, :, width:].reshape(count, LANES).astype(F32)
    total = jnp.sum(tail, 1, keepdims=True) / jnp.where(gate > 0, gate, 1.0)
    lane = lax.broadcasted_iota(jnp.int32, (count, LANES), 1).astype(F32)
    spread = jnp.zeros((count, LANES), F32)
    for index, part in enumerate(split3(total)):
        spread = jnp.where(lane == slot_place[...] + float(index * top), part.astype(F32), spread)
    tail = dot(pick[...], spread.astype(BF16), 0, 0).astype(BF16)
    spread_blocks(blocks, tail, slice(width, wide))


def along(value, sign):
    size = lax.axis_size("z")
    pairs = []
    for z in range(size):
        pairs.append((2 * z, 2 * ((z + sign) % size)))
        pairs.append((2 * z + 1, 2 * ((z - sign) % size) + 1))
    return lax.ppermute(value, ("z", "c"), pairs)


def swap(value):
    return lax.ppermute(value, "c", [(0, 1), (1, 0)])


def ring_gather(block, pair):
    far = lax.axis_size("z") // 2
    blocks = [block]
    moving = pair
    for step in range(far):
        moving = along(moving if step < far - 1 else moving[: block.shape[0]], 1)
        blocks.append(moving)
    return blocks


def add(left, right):
    return (left.astype(F32) + right.astype(F32)).astype(BF16)


def ring_reduce(blocks, after=None):
    rows = blocks[0].shape[0]
    far = len(blocks) - 1
    hop = along(blocks[far], -1)
    arrived = [along(blocks[step], -step) for step in range(1, far - 1)]
    last = add(blocks[far - 1], jnp.pad(hop, ((0, rows), (0, 0))))
    arrived.append(along(last, 1 - far))
    if after is not None:
        *arrived, _ = lax.optimization_barrier((*arrived, after))
    both = sum(value.astype(F32) for value in arrived)
    other = swap(both[rows:].astype(BF16))
    return blocks[0].astype(F32) + both[:rows] + other.astype(F32)


def merge_kernel(first_0, relayed_0, second_0, first_1, relayed_1, second_1, joined_0, joined_1):
    rows = first_0.shape[0]
    joined_0[:rows, :] = (first_0[...].astype(F32) + relayed_0[...].astype(F32)).astype(BF16)
    joined_0[rows:, :] = second_0[...]
    joined_1[:rows, :] = (first_1[...].astype(F32) + relayed_1[...].astype(F32)).astype(BF16)
    joined_1[rows:, :] = second_1[...]


def touch_kernel(left, right, left_out, right_out):
    del left, right, left_out, right_out


def touch(left, right, name):
    return pl.pallas_call(
        touch_kernel,
        out_shape=[jax.ShapeDtypeStruct(v.shape, v.dtype) for v in (left, right)],
        in_specs=[ANY] * 2,
        out_specs=[ANY] * 2,
        input_output_aliases={0: 0, 1: 1},
        cost_estimate=pl.CostEstimate(
            flops=COST[name] * 10**9, bytes_accessed=0, transcendentals=0
        ),
        name=name,
    )(left, right)


def final_kernel(own_0, own_1, before, after, gate_up_grad, down_grad):
    rows = own_0.shape[0]
    half = rows // 3
    for side, own in ((0, own_0), (1, own_1)):
        units = slice(side * half, (side + 1) * half)
        for kind in range(3):
            span = slice(kind * half, (kind + 1) * half)
            up = slice(side * rows + kind * half, side * rows + (kind + 1) * half)
            down = slice((1 - side) * rows + kind * half, (1 - side) * rows + (kind + 1) * half)
            total = own[span, :].astype(F32) + before[up, :].astype(F32)
            total = total + after[down, :].astype(F32)
            if kind < 2:
                gate_up_grad[0, units, kind, :] = total
            else:
                down_grad[0, units, :] = total


def body(tokens, expert_ids, route_gates, gate_up, down_weight, out_grad):
    tok_count, width = tokens.shape
    top = expert_ids.shape[1]
    z_size = lax.axis_size("z")
    dests = lax.axis_size("x") * 2
    cap = 6 * z_size
    count = dests * cap
    held = tok_count * z_size
    units = gate_up.shape[1]
    half = units // 2
    wide = width + LANES
    n = 8
    full = n * half

    three = 3 * half
    (own,) = call(
        weights_kernel,
        [((2 * three, width), BF16)],
        [strips(gate_up.shape), strips(down_weight.shape)],
        [strips((2 * three, width))],
        [],
        0,
        0,
        MIB,
        "weights",
        (width // TILE,),
    )(gate_up, down_weight)
    tokens, _ = lax.optimization_barrier((tokens, own))
    before = shift(own, "dp", 1)
    after = shift(own, "dp", -1)
    (packed,) = call(
        pack_kernel, [((tok_count, wide), BF16)], [VMEM] * 3, [VMEM], [], 0, 0, MIB, "pack"
    )(tokens, expert_ids.T, route_gates.T)
    pair = jnp.concatenate([packed, swap(packed)], 0)
    grad_pair = jnp.concatenate([out_grad, swap(out_grad)], 0)
    blocks = ring_gather(packed, pair)
    grad_blocks = ring_gather(out_grad, grad_pair)
    z_index = lax.axis_index("z").astype(jnp.int32).reshape(1)
    rows_type = ((dests, cap, width), BF16)
    pick_flops = 2 * count * held * width
    send, pick, slot_gate, slot_place = call(
        functools.partial(select_kernel, top, dests, cap),
        [((dests, 2 * cap, width), BF16), ((count, held), BF16)] + [((count, LANES), F32)] * 2,
        [SMEM] + [VMEM] * (2 * len(blocks)),
        [VMEM] * 4,
        [pltpu.VMEM((held, wide), BF16), pltpu.VMEM((held, width), BF16)],
        pick_flops,
        3 * 10**6,
        MIB,
        "select",
    )(z_index, *blocks, *grad_blocks)
    before, _ = lax.optimization_barrier((before, send))
    after, _ = lax.optimization_barrier((after, send))
    far_0 = shift(before[:three], "dp", 1)
    far_1 = shift(after[three:], "dp", -1)
    far_0, far_1 = touch(far_0, far_1, "touch")
    pieces = [own, before, after, far_0, far_1]

    arrived = lax.all_to_all(send, ("x", "c"), 0, 0, tiled=True)

    shards = n // 2 - 1
    hidden_type = ((count, units), BF16)
    piece_type = ((3 * half, width), BF16)
    weight = pltpu.VMEM((full, width), BF16)
    held_types = [((shards, count, units), F32)] * 2 + [((shards, count, units), BF16), rows_type]
    held_types = held_types + [piece_type] * 2
    gate_all, up_all, hid, result, far_g0, far_g1, gcot_f, ucot_f, score_f = call(
        forward_kernel,
        held_types + [hidden_type, hidden_type, ((count, LANES), F32)],
        [ANY] * (1 + len(pieces)),
        [ANY] * 6 + [VMEM] * 3,
        [pltpu.VMEM(s, d) for s, d in held_types]
        + [pltpu.VMEM((dests, 2 * cap, width), BF16)]
        + [pltpu.VMEM((count, units), BF16), pltpu.VMEM((3, units, count), BF16)]
        + [weight] * 3
        + [pltpu.SemaphoreType.DMA((k,)) for k in (3 * n, 1, 6)],
        1,
        0,
        MIB,
        "forward",
    )(arrived, *pieces)
    result_cot, own_0, own_1, before_g0, before_g1, after_g0, after_g1 = call(
        backward_kernel,
        [((dests, cap, wide), BF16)] + [piece_type] * (n - 2),
        [VMEM] * 7 + [ANY] * len(pieces),
        [VMEM] * (n - 1),
        [pltpu.VMEM((shards, count, units), BF16)] * 2
        + [pltpu.VMEM((3, units * shards, count), BF16)]
        + [weight] * 3
        + [pltpu.SemaphoreType.DMA((3 * n - 2,))],
        1,
        0,
        MIB,
        "backward",
    )(arrived, gate_all, up_all, hid, gcot_f, ucot_f, score_f, *pieces)

    relay_0 = shift(far_g0, "dp", 1)
    relay_1 = shift(far_g1, "dp", -1)

    joined_0, joined_1 = call(
        merge_kernel,
        [((2 * three, width), BF16)] * 2,
        [strips((three, width))] * 6,
        [strips((2 * three, width))] * 2,
        [],
        1,
        0,
        MIB,
        "merge",
        (width // TILE,),
    )(after_g0, relay_0, after_g1, before_g1, relay_1, before_g0)
    got_before = shift(joined_0, "dp", 1)
    got_after = shift(joined_1, "dp", -1)
    got_before, got_after = touch(got_before, got_after, "touch2")
    gate_up_grad, down_grad = call(
        final_kernel,
        [(gate_up.shape, F32), (down_weight.shape, F32)],
        [strips((three, width))] * 2 + [strips((2 * three, width))] * 2,
        [strips(gate_up.shape), strips(down_weight.shape)],
        [],
        0,
        0,
        MIB,
        "final",
        (width // TILE,),
    )(own_0, own_1, got_before, got_after)

    back = lax.all_to_all(result, ("x", "c"), 0, 0, tiled=True)
    parts = call(
        combine_kernel,
        [((b.shape[0], width), BF16) for b in blocks],
        [VMEM] * 3 + [ANY],
        [VMEM] * len(blocks),
        [],
        pick_flops,
        3 * 10**6,
        MIB,
        "combine",
    )(back, pick, slot_gate, joined_0)
    moe_out = ring_reduce(list(parts)).astype(BF16)
    back_cot = lax.all_to_all(result_cot, ("x", "c"), 0, 0, tiled=True)
    parts = call(
        functools.partial(combine_cot_kernel, top),
        [((b.shape[0], wide), BF16) for b in blocks],
        [VMEM] * 4,
        [VMEM] * len(blocks),
        [],
        pick_flops,
        3 * 10**6,
        MIB,
        "combine_cot",
    )(back_cot, pick, slot_gate, slot_place)
    summed = ring_reduce(list(parts), down_grad)
    token_grad = summed[:, :width].astype(BF16)
    tail = summed[:, width:]
    gate_grad = tail[:, :top] + tail[:, top : 2 * top] + tail[:, 2 * top : 3 * top]
    return moe_out, gate_grad, token_grad, gate_up_grad, down_grad


def solution(mesh):
    wide = Mesh(mesh.devices.reshape(4, 4, 8, 2), ("dp", "x", "z", "c"))
    expert = ("x", "z", "c")
    every = ("dp",) + expert
    in_specs = (
        P(every, None),
        P(every, None),
        P(every, None),
        P(expert, "dp", None, None),
        P(expert, "dp", None),
        P(every, None),
    )
    out_specs = (
        P(every, None),
        P(every, None),
        P(every, None),
        P(expert, "dp", None, None),
        P(expert, "dp", None),
    )
    return jax.shard_map(body, mesh=wide, in_specs=in_specs, out_specs=out_specs, check_vma=False)
```

```python
import functools

import jax
import jax.numpy as jnp
from jax import lax
from jax.experimental import pallas as pl
from jax.experimental.pallas import tpu as pltpu
from jax.sharding import Mesh
from jax.sharding import PartitionSpec as P

F32 = jnp.float32
BF16 = jnp.bfloat16
LANES = 128
TILE = 1024
WIDE = 2048
PIECES = 5
PLACES = ((0, 0), (0, 3), (1, 0), (1, 3), (2, 0), (2, 3), (3, 0), (4, 0))
MIB = 56
COST = {"pack": 0, "touch2": 0, "weights": 10, "select": 0, "merge": 80, "combine": 0, "combine_cot": 0, "forward": 1, "backward": 1, "final": 0, "touch": 10}
VMEM = pl.BlockSpec(memory_space=pltpu.VMEM)
SMEM = pl.BlockSpec(memory_space=pltpu.SMEM)
ANY = pl.BlockSpec(memory_space=pl.ANY)


def shift(value, axis, step):
    size = lax.axis_size(axis)
    return lax.ppermute(value, axis, [(i, (i + step) % size) for i in range(size)])


def dot(left, right, left_dim, right_dim):
    return lax.dot_general(
        left, right, (((left_dim,), (right_dim,)), ((), ())), preferred_element_type=F32
    )


def call(kernel, outs, in_specs, out_specs, scratch, flops, bytes_accessed, mib, name, grid=()):
    return pl.pallas_call(
        kernel,
        grid=grid,
        out_shape=[jax.ShapeDtypeStruct(s, d) for s, d in outs],
        in_specs=in_specs,
        out_specs=out_specs,
        scratch_shapes=scratch,
        compiler_params=pltpu.CompilerParams(vmem_limit_bytes=mib * 1024 * 1024),
        cost_estimate=pl.CostEstimate(
            flops=COST[name] * 10**9, bytes_accessed=0, transcendentals=0
        ),
        name=name,
    )


def strips(shape):
    lead = len(shape) - 1
    return pl.BlockSpec(tuple(shape[:-1]) + (TILE,), lambda step: (0,) * lead + (step,))


def split3(value):
    high = value.astype(BF16)
    rest = value - high.astype(F32)
    middle = rest.astype(BF16)
    low = (rest - middle.astype(F32)).astype(BF16)
    return high, middle, low


def pack_kernel(tokens, ids, gates, grads, packed, grads_out):
    width = tokens.shape[1]
    top = ids.shape[0]
    row = lax.broadcasted_iota(jnp.int32, (top, LANES), 0)
    lane = lax.broadcasted_iota(jnp.int32, (top, LANES), 1)
    fields = (ids[...].astype(F32).astype(BF16),) + split3(gates[...])
    tail = jnp.zeros((tokens.shape[0], LANES), F32)
    for index, field in enumerate(fields):
        place = (lane == row + index * top).astype(F32).astype(BF16)
        tail = tail + dot(field, place, 0, 0)
    packed[:, :width] = tokens[...]
    packed[:, width:] = tail.astype(BF16)
    grads_out[...] = grads[...]


def weights_kernel(gate_up, down, own):
    half = own.shape[0] // 6
    for part in range(2):
        units = slice(part * half, (part + 1) * half)
        first = 3 * part * half
        for kind in range(2):
            rows = slice(first + kind * half, first + (kind + 1) * half)
            own[rows, :] = gate_up[0, units, kind, :]
        own[first + 2 * half : first + 3 * half, :] = down[0, units, :]


def gather_blocks(blocks, held):
    first = 0
    for block in blocks:
        held[first : first + block.shape[0], :] = block[...]
        first += block.shape[0]


def select_kernel(top, dests, cap, z_index, *refs):
    blocks, grad_blocks = refs[:5], refs[5:10]
    send, pick_out, gate_out, place_out, held, held_grads = refs[-6:]
    width = send.shape[2]
    count = held.shape[0]
    gather_blocks(blocks, held)
    gather_blocks(grad_blocks, held_grads)
    info = held[:, width:].astype(F32).T
    ids = info[:top]
    gates = info[top : 2 * top] + info[2 * top : 3 * top] + info[3 * top : 4 * top]
    order = lax.broadcasted_iota(jnp.int32, (top, count), 0).astype(F32)
    base = (z_index[0] * 2).astype(F32)
    marks, gate_rows, place_rows = [], [], []
    for dest in range(dests):
        expert = base + float((dest // 2) * 16 + dest % 2)
        chosen = ids == expert
        marks.append(jnp.sum(jnp.where(chosen, 1.0, 0.0), 0, keepdims=True))
        gate_rows.append(jnp.sum(jnp.where(chosen, gates, 0.0), 0, keepdims=True))
        place_rows.append(jnp.sum(jnp.where(chosen, order, 0.0), 0, keepdims=True))
    mark = jnp.concatenate(marks, 0)
    before = lax.broadcasted_iota(jnp.int32, (count, count), 0) < lax.broadcasted_iota(
        jnp.int32, (count, count), 1
    )
    rank = dot(mark.astype(BF16), before.astype(F32).astype(BF16), 1, 0)
    rank = jnp.where(mark > 0, rank, -1.0)
    slot = lax.broadcasted_iota(jnp.int32, (cap, count), 0).astype(F32)
    slot_gates = []
    for dest in range(dests):
        span = slice(dest * cap, (dest + 1) * cap)
        hit = rank[dest : dest + 1] == slot
        pick_out[span, :] = jnp.where(hit, 1.0, 0.0).astype(BF16)
        slot_gate = jnp.sum(jnp.where(hit, gate_rows[dest], 0.0), 1, keepdims=True)
        slot_place = jnp.sum(jnp.where(hit, place_rows[dest], 0.0), 1, keepdims=True)
        gate_out[span, :] = jnp.broadcast_to(slot_gate, (cap, LANES))
        place_out[span, :] = jnp.broadcast_to(slot_place, (cap, LANES))
        slot_gates.append(slot_gate)
    slot_gate = jnp.concatenate(slot_gates, 0)

    def columns(step, carry):
        span = pl.ds(pl.multiple_of(step * WIDE, WIDE), WIDE)
        tok = dot(pick_out[...], held[:, span], 1, 0).astype(BF16)
        send[:, :cap, span] = tok.reshape(dests, cap, WIDE)
        cot = slot_gate * dot(pick_out[...], held_grads[:, span], 1, 0)
        send[:, cap:, span] = cot.astype(BF16).reshape(dests, cap, WIDE)
        return carry

    lax.fori_loop(0, width // WIDE, columns, 0)


def load(pieces, places, weights, sems, skip=0):
    half = pieces[-1].shape[0] // 3
    copies = []
    for index, (number, first) in enumerate(places):
        group = []
        for slot, (kind, weight) in enumerate(weights):
            copy = pltpu.make_async_copy(
                pieces[number].at[pl.ds(first * half + kind * half, half), :],
                weight.at[pl.ds((index + skip) * half, half), :],
                sems.at[index * len(weights) + slot],
            )
            copy.start()
            group.append(copy)
        copies.append(group)
    return copies


def wait_all(copies):
    for group in copies:
        for copy in group:
            copy.wait()


def hidden_parts(gate_pre, up_pre, hidden_cot):
    sigma = jax.nn.sigmoid(gate_pre)
    gate_cot = hidden_cot * up_pre * sigma * (1.0 + gate_pre * (1.0 - sigma))
    return gate_cot, hidden_cot * (gate_pre * sigma)


def fold(value):
    wide = jnp.concatenate([value, jnp.zeros((value.shape[0], 64), F32)], 1)
    return wide[:, :LANES] + wide[:, LANES:]


def forward_kernel(arrived_hbm, *refs):
    pieces = refs[:PIECES]
    outs = refs[PIECES : PIECES + 6]
    gcot, ucot, score = refs[PIECES + 6 : PIECES + 9]
    held = refs[PIECES + 9 : PIECES + 15]
    gate_all, up_all, hid, result, grad_0, grad_1 = held
    arrived, hid_far, lefts, w_gate, w_up, w_down, sems, in_sems, out_sems = refs[PIECES + 15 :]
    dests, double, width = arrived.shape
    cap = double // 2
    count = dests * cap
    half = grad_0.shape[0] // 3
    shards = len(PLACES) // 2
    kinds = ((0, w_gate), (1, w_up), (2, w_down))
    arrival = pltpu.make_async_copy(arrived_hbm, arrived, in_sems.at[0])
    arrival.start()
    copies = load(pieces, PLACES[-2:], kinds, sems.at[pl.ds(0, 6)])
    arrival.wait()
    wait_all(copies)
    near = len(PLACES) - 2
    copies = load(pieces, PLACES[:-2], kinds, sems.at[pl.ds(6, 3 * near)], 2)
    rows = arrived[:, :cap, :].reshape(count, width)
    leaving = []

    def leave(index):
        copy = pltpu.make_async_copy(held[index], outs[index], out_sems.at[index])
        copy.start()
        leaving.append(copy)

    hidden = []
    for shard in range(shards):
        if shard:
            wait_all(copies[2 * shard - 2 : 2 * shard])
        span = slice(2 * shard * half, 2 * (shard + 1) * half)
        gate_pre = dot(rows, w_gate[span, :], 1, 1)
        up_pre = dot(rows, w_up[span, :], 1, 1)
        value = (gate_pre * jax.nn.sigmoid(gate_pre) * up_pre).astype(BF16)
        if shard:
            gate_all[shard - 1], up_all[shard - 1], hid[shard - 1] = gate_pre, up_pre, value
            hidden.append(hid.at[shard - 1])
            continue
        hid_far[...] = value
        hidden.append(hid_far)
        hidden_cot = dot(arrived[:, cap:, :].reshape(count, width), w_down[span, :], 1, 1)
        gate_cot, up_cot = hidden_parts(gate_pre, up_pre, hidden_cot)
        gcot[...] = gate_cot.astype(BF16)
        ucot[...] = up_cot.astype(BF16)
        score[...] = fold(value.astype(F32) * hidden_cot)
        lefts[0] = gate_cot.T.astype(BF16)
        lefts[1] = up_cot.T.astype(BF16)
        lefts[2] = value.astype(F32).T.astype(BF16)
        write_grads(arrived, lefts, (grad_0, grad_1))
        leave(4)
        leave(5)
    for index in range(3):
        leave(index)

    def columns(step, carry):
        span = pl.ds(pl.multiple_of(step * TILE, TILE), TILE)
        out = jnp.zeros((count, TILE), F32)
        for shard, value in enumerate(hidden):
            units = slice(2 * shard * half, 2 * (shard + 1) * half)
            out = out + dot(value[...], w_down[units, span], 1, 0)
        result[:, :, span] = out.astype(BF16).reshape(dests, cap, TILE)
        return carry

    lax.fori_loop(0, width // TILE, columns, 0)
    leave(3)
    for copy in leaving:
        copy.wait()


def write_grads(arrived, lefts, pieces):
    dests, double, width = arrived.shape
    cap = double // 2
    count = dests * cap
    half = pieces[0].shape[0] // 3

    def columns(step, carry):
        span = pl.ds(pl.multiple_of(step * TILE, TILE), TILE)
        rows = arrived[:, :cap, span].reshape(count, TILE)
        cots = arrived[:, cap:, span].reshape(count, TILE)
        for kind, right in enumerate((rows, rows, cots)):
            grad = dot(lefts[kind], right, 1, 0).astype(BF16)
            for index, piece in enumerate(pieces):
                piece[kind * half : (kind + 1) * half, span] = grad[
                    index * half : (index + 1) * half
                ]
        return carry

    lax.fori_loop(0, width // TILE, columns, 0)


def backward_kernel(arrived, gate_all, up_all, hid, gcot_far, ucot_far, score_far, *refs):
    pieces = refs[:PIECES]
    near = len(PLACES) - 2
    result = refs[PIECES]
    grads = refs[PIECES + 1 : PIECES + 1 + near]
    gcot, ucot, lefts, w_gate, w_up, w_down, sems = refs[PIECES + 1 + near :]
    dests, double, width = arrived.shape
    cap = double // 2
    count = dests * cap
    half = grads[0].shape[0] // 3
    copies = load(pieces, PLACES[:near], ((2, w_down),), sems.at[pl.ds(0, near)])
    others = load(pieces, PLACES, ((0, w_gate), (1, w_up)), sems.at[pl.ds(near, 2 * near + 4)])
    cots = arrived[:, cap:, :].reshape(count, width)
    score = score_far[...]
    for shard in range(near // 2):
        wait_all(copies[2 * shard : 2 * shard + 2])
        span = slice(2 * shard * half, 2 * (shard + 1) * half)
        hidden_cot = dot(cots, w_down[span, :], 1, 1)
        hidden = hid[shard].astype(F32)
        gate_cot, up_cot = hidden_parts(gate_all[shard], up_all[shard], hidden_cot)
        gcot[shard] = gate_cot.astype(BF16)
        ucot[shard] = up_cot.astype(BF16)
        lefts[0, span, :] = gate_cot.T.astype(BF16)
        lefts[1, span, :] = up_cot.T.astype(BF16)
        lefts[2, span, :] = hidden.T.astype(BF16)
        score = score + fold(hidden * hidden_cot)
    total = jnp.sum(score, 1, keepdims=True)
    lane = lax.broadcasted_iota(jnp.int32, (count, LANES), 1)
    high, middle, low = (part.astype(F32) for part in split3(total))
    tail = jnp.where(lane == 0, high, jnp.where(lane == 1, middle, jnp.where(lane == 2, low, 0.0)))
    result[:, :, width:] = tail.astype(BF16).reshape(dests, cap, LANES)
    write_grads(arrived, lefts, grads)
    wait_all(others)

    def columns(step, carry):
        span = pl.ds(pl.multiple_of(step * TILE, TILE), TILE)
        first = half * near
        dx = dot(gcot_far[...], w_gate[first:, span], 1, 0)
        dx = dx + dot(ucot_far[...], w_up[first:, span], 1, 0)
        for shard in range(near // 2):
            units = slice(2 * shard * half, 2 * (shard + 1) * half)
            dx = dx + dot(gcot[shard], w_gate[units, span], 1, 0)
            dx = dx + dot(ucot[shard], w_up[units, span], 1, 0)
        result[:, :, span] = dx.astype(BF16).reshape(dests, cap, TILE)
        return carry

    lax.fori_loop(0, width // TILE, columns, 0)


def spread_blocks(blocks, value, span):
    first = 0
    for block in blocks:
        block[:, span] = value[first : first + block.shape[0]]
        first += block.shape[0]


def combine_kernel(back, pick, slot_gate, joined, *blocks):
    del joined
    dests, cap, width = back.shape

    def columns(step, carry):
        span = pl.ds(pl.multiple_of(step * WIDE, WIDE), WIDE)
        out = back[:, :, span].reshape(dests * cap, WIDE).astype(F32)
        weighted = (slot_gate[:, :1] * out).astype(BF16)
        spread_blocks(blocks, dot(pick[...], weighted, 0, 0).astype(BF16), span)
        return carry

    lax.fori_loop(0, width // WIDE, columns, 0)


def combine_cot_kernel(top, back, pick, slot_gate, slot_place, *blocks):
    dests, cap, wide = back.shape
    width = wide - LANES
    count = dests * cap
    gate = slot_gate[:, :1]

    def columns(step, carry):
        span = pl.ds(pl.multiple_of(step * WIDE, WIDE), WIDE)
        dx = back[:, :, span].reshape(count, WIDE)
        spread_blocks(blocks, dot(pick[...], dx, 0, 0).astype(BF16), span)
        return carry

    lax.fori_loop(0, width // WIDE, columns, 0)
    tail = back[:, :, width:].reshape(count, LANES).astype(F32)
    total = jnp.sum(tail, 1, keepdims=True) / jnp.where(gate > 0, gate, 1.0)
    lane = lax.broadcasted_iota(jnp.int32, (count, LANES), 1).astype(F32)
    spread = jnp.zeros((count, LANES), F32)
    for index, part in enumerate(split3(total)):
        spread = jnp.where(lane == slot_place[...] + float(index * top), part.astype(F32), spread)
    tail = dot(pick[...], spread.astype(BF16), 0, 0).astype(BF16)
    spread_blocks(blocks, tail, slice(width, wide))


def along(value, sign):
    size = lax.axis_size("z")
    pairs = []
    for z in range(size):
        pairs.append((2 * z, 2 * ((z + sign) % size)))
        pairs.append((2 * z + 1, 2 * ((z - sign) % size) + 1))
    return lax.ppermute(value, ("z", "c"), pairs)


def swap(value):
    return lax.ppermute(value, "c", [(0, 1), (1, 0)])


def ring_gather(block, pair):
    far = lax.axis_size("z") // 2
    blocks = [block]
    moving = pair
    for step in range(far):
        moving = along(moving if step < far - 1 else moving[: block.shape[0]], 1)
        blocks.append(moving)
    return blocks


def add(left, right):
    return (left.astype(F32) + right.astype(F32)).astype(BF16)


def ring_reduce(blocks, after=None):
    rows = blocks[0].shape[0]
    far = len(blocks) - 1
    hop = along(blocks[far], -1)
    arrived = [along(blocks[step], -step) for step in range(1, far - 1)]
    last = add(blocks[far - 1], jnp.pad(hop, ((0, rows), (0, 0))))
    arrived.append(along(last, 1 - far))
    if after is not None:
        *arrived, _ = lax.optimization_barrier((*arrived, after))
    both = sum(value.astype(F32) for value in arrived)
    other = swap(both[rows:].astype(BF16))
    return blocks[0].astype(F32) + both[:rows] + other.astype(F32)


def merge_kernel(first_0, relayed_0, second_0, first_1, relayed_1, second_1, joined_0, joined_1):
    rows = first_0.shape[0]
    joined_0[:rows, :] = (first_0[...].astype(F32) + relayed_0[...].astype(F32)).astype(BF16)
    joined_0[rows:, :] = second_0[...]
    joined_1[:rows, :] = (first_1[...].astype(F32) + relayed_1[...].astype(F32)).astype(BF16)
    joined_1[rows:, :] = second_1[...]


def touch_kernel(left, right, left_out, right_out):
    del left, right, left_out, right_out


def touch(left, right, name):
    return pl.pallas_call(
        touch_kernel,
        out_shape=[jax.ShapeDtypeStruct(v.shape, v.dtype) for v in (left, right)],
        in_specs=[ANY] * 2,
        out_specs=[ANY] * 2,
        input_output_aliases={0: 0, 1: 1},
        cost_estimate=pl.CostEstimate(
            flops=COST[name] * 10**9, bytes_accessed=0, transcendentals=0
        ),
        name=name,
    )(left, right)


def final_kernel(own_0, own_1, before, after, gate_up_grad, down_grad):
    rows = own_0.shape[0]
    half = rows // 3
    for side, own in ((0, own_0), (1, own_1)):
        units = slice(side * half, (side + 1) * half)
        for kind in range(3):
            span = slice(kind * half, (kind + 1) * half)
            up = slice(side * rows + kind * half, side * rows + (kind + 1) * half)
            down = slice((1 - side) * rows + kind * half, (1 - side) * rows + (kind + 1) * half)
            total = own[span, :].astype(F32) + before[up, :].astype(F32)
            total = total + after[down, :].astype(F32)
            if kind < 2:
                gate_up_grad[0, units, kind, :] = total
            else:
                down_grad[0, units, :] = total


def body(tokens, expert_ids, route_gates, gate_up, down_weight, out_grad):
    tok_count, width = tokens.shape
    top = expert_ids.shape[1]
    z_size = lax.axis_size("z")
    dests = lax.axis_size("x") * 2
    cap = 6 * z_size
    count = dests * cap
    held = tok_count * z_size
    units = gate_up.shape[1]
    half = units // 2
    wide = width + LANES
    n = 8
    full = n * half

    three = 3 * half
    (own,) = call(
        weights_kernel,
        [((2 * three, width), BF16)],
        [strips(gate_up.shape), strips(down_weight.shape)],
        [strips((2 * three, width))],
        [],
        0,
        0,
        MIB,
        "weights",
        (width // TILE,),
    )(gate_up, down_weight)
    tokens, _ = lax.optimization_barrier((tokens, own))
    before = shift(own, "dp", 1)
    after = shift(own, "dp", -1)
    packed, out_grad = call(
        pack_kernel,
        [((tok_count, wide), BF16), ((tok_count, width), BF16)],
        [VMEM] * 4,
        [VMEM] * 2,
        [],
        0,
        0,
        MIB,
        "pack",
    )(tokens, expert_ids.T, route_gates.T, out_grad)
    pair = jnp.concatenate([packed, swap(packed)], 0)
    grad_pair = jnp.concatenate([out_grad, swap(out_grad)], 0)
    blocks = ring_gather(packed, pair)
    grad_blocks = ring_gather(out_grad, grad_pair)
    z_index = lax.axis_index("z").astype(jnp.int32).reshape(1)
    rows_type = ((dests, cap, width), BF16)
    pick_flops = 2 * count * held * width
    send, pick, slot_gate, slot_place = call(
        functools.partial(select_kernel, top, dests, cap),
        [((dests, 2 * cap, width), BF16), ((count, held), BF16)] + [((count, LANES), F32)] * 2,
        [SMEM] + [VMEM] * (2 * len(blocks)),
        [VMEM] * 4,
        [pltpu.VMEM((held, wide), BF16), pltpu.VMEM((held, width), BF16)],
        pick_flops,
        3 * 10**6,
        MIB,
        "select",
    )(z_index, *blocks, *grad_blocks)
    before, _ = lax.optimization_barrier((before, send))
    after, _ = lax.optimization_barrier((after, send))
    far_0 = shift(before[:three], "dp", 1)
    far_1 = shift(after[three:], "dp", -1)
    far_0, far_1 = touch(far_0, far_1, "touch")
    pieces = [own, before, after, far_0, far_1]

    arrived = lax.all_to_all(send, ("x", "c"), 0, 0, tiled=True)

    shards = n // 2 - 1
    hidden_type = ((count, units), BF16)
    piece_type = ((3 * half, width), BF16)
    weight = pltpu.VMEM((full, width), BF16)
    held_types = [((shards, count, units), F32)] * 2 + [((shards, count, units), BF16), rows_type]
    held_types = held_types + [piece_type] * 2
    gate_all, up_all, hid, result, far_g0, far_g1, gcot_f, ucot_f, score_f = call(
        forward_kernel,
        held_types + [hidden_type, hidden_type, ((count, LANES), F32)],
        [ANY] * (1 + len(pieces)),
        [ANY] * 6 + [VMEM] * 3,
        [pltpu.VMEM(s, d) for s, d in held_types]
        + [pltpu.VMEM((dests, 2 * cap, width), BF16)]
        + [pltpu.VMEM((count, units), BF16), pltpu.VMEM((3, units, count), BF16)]
        + [weight] * 3
        + [pltpu.SemaphoreType.DMA((k,)) for k in (3 * n, 1, 6)],
        1,
        0,
        MIB,
        "forward",
    )(arrived, *pieces)
    result_cot, own_0, own_1, before_g0, before_g1, after_g0, after_g1 = call(
        backward_kernel,
        [((dests, cap, wide), BF16)] + [piece_type] * (n - 2),
        [VMEM] * 7 + [ANY] * len(pieces),
        [VMEM] * (n - 1),
        [pltpu.VMEM((shards, count, units), BF16)] * 2
        + [pltpu.VMEM((3, units * shards, count), BF16)]
        + [weight] * 3
        + [pltpu.SemaphoreType.DMA((3 * n - 2,))],
        1,
        0,
        MIB,
        "backward",
    )(arrived, gate_all, up_all, hid, gcot_f, ucot_f, score_f, *pieces)

    relay_0 = shift(far_g0, "dp", 1)
    relay_1 = shift(far_g1, "dp", -1)

    joined_0, joined_1 = call(
        merge_kernel,
        [((2 * three, width), BF16)] * 2,
        [strips((three, width))] * 6,
        [strips((2 * three, width))] * 2,
        [],
        1,
        0,
        MIB,
        "merge",
        (width // TILE,),
    )(after_g0, relay_0, after_g1, before_g1, relay_1, before_g0)
    got_before = shift(joined_0, "dp", 1)
    got_after = shift(joined_1, "dp", -1)
    got_before, got_after = touch(got_before, got_after, "touch2")
    gate_up_grad, down_grad = call(
        final_kernel,
        [(gate_up.shape, F32), (down_weight.shape, F32)],
        [strips((three, width))] * 2 + [strips((2 * three, width))] * 2,
        [strips(gate_up.shape), strips(down_weight.shape)],
        [],
        0,
        0,
        MIB,
        "final",
        (width // TILE,),
    )(own_0, own_1, got_before, got_after)

    back = lax.all_to_all(result, ("x", "c"), 0, 0, tiled=True)
    parts = call(
        combine_kernel,
        [((b.shape[0], width), BF16) for b in blocks],
        [VMEM] * 3 + [ANY],
        [VMEM] * len(blocks),
        [],
        pick_flops,
        3 * 10**6,
        MIB,
        "combine",
    )(back, pick, slot_gate, joined_0)
    moe_out = ring_reduce(list(parts)).astype(BF16)
    back_cot = lax.all_to_all(result_cot, ("x", "c"), 0, 0, tiled=True)
    parts = call(
        functools.partial(combine_cot_kernel, top),
        [((b.shape[0], wide), BF16) for b in blocks],
        [VMEM] * 4,
        [VMEM] * len(blocks),
        [],
        pick_flops,
        3 * 10**6,
        MIB,
        "combine_cot",
    )(back_cot, pick, slot_gate, slot_place)
    summed = ring_reduce(list(parts), down_grad)
    token_grad = summed[:, :width].astype(BF16)
    tail = summed[:, width:]
    gate_grad = tail[:, :top] + tail[:, top : 2 * top] + tail[:, 2 * top : 3 * top]
    return moe_out, gate_grad, token_grad, gate_up_grad, down_grad


def solution(mesh):
    wide = Mesh(mesh.devices.reshape(4, 4, 8, 2), ("dp", "x", "z", "c"))
    expert = ("x", "z", "c")
    every = ("dp",) + expert
    in_specs = (
        P(every, None),
        P(every, None),
        P(every, None),
        P(expert, "dp", None, None),
        P(expert, "dp", None),
        P(every, None),
    )
    out_specs = (
        P(every, None),
        P(every, None),
        P(every, None),
        P(expert, "dp", None, None),
        P(expert, "dp", None),
    )
    return jax.shard_map(body, mesh=wide, in_specs=in_specs, out_specs=out_specs, check_vma=False)
```
